512 devices in a mesh: grp: 8 (over x, core), leaf: 64 (over z, y).
Axes of the slice: x: 4, y: 8, z: 8, core: 2. Of those that a mesh axis runs over, the one named last changes fastest.
Arguments:
- self_blocks: bfloat16 [1024, 512, 512], P(('grp', 'leaf')), as said below
- near_blocks: bfloat16 [1024, 1, 512, 512], P(('grp', 'leaf')), may hold values from -6 to 6
- leaf_basis: bfloat16 [1024, 512, 512], P(('grp', 'leaf')), may hold values from -0.25 to 0.25
- transfer: bfloat16 [1024, 16, 128, 128], P(('grp', 'leaf')), may hold values from -0.5 to 0.5
- near_list: int32 [1024, 1], P(('grp', 'leaf')), may hold values from 0 to 1023, as said below
- adm_list: int32 [1024, 16], P(('grp', 'leaf')), may hold values from 0 to 63, all different within a row; in each aligned block of 2 rows (0 to 1, 2 to 3, ...) at most 2 rows name the same one
- parent_kernel: bfloat16 [512, 128, 128], P(('grp', 'leaf')), may hold values from -0.00390625 to 0.00390625
- chain_coupling: float32 [8, 128, 128], P('grp'), may hold values from -0.5 to 0.5
Outputs:
- leaf_panels: float32 [1024, 128, 128], P(('grp', 'leaf'))
- parent_panels: float32 [512, 128, 128], P(('grp', 'leaf'))
- top_panels: float32 [8, 128, 128], P('grp')
The draws below stay inside these ranges and needn't reach their ends.
Inputs may be any that keep to these rules, and one draw needn't show every extreme that they name: self_blocks are symmetric and strictly diagonally dominant with positive diagonal. `near_list`: each entry names a leaf held by a device next to the leaf's own device along leaf, in the same subtree. `adm_list`: each leaf names 16 different parents of its own subtree; parent p of a subtree is held by the device at place p along leaf; some parents are named far more often than others.
All inputs are finite; a program needn't handle non-finite values.
Results may differ from the reference program's by a relative error of at most 0.012.
Values may be sent and summed in bfloat16 or wider, within the bound.
A program may use at most 64 MiB of HBM per device.

```python
import math
import jax
import jax.numpy as jnp
import numpy as np
from jax import lax

LEAF_SIZE = 512
SKELETON = 128
REDUNDANT = 384
LEAF_DEV = 2
NEAR_LINKS = 1
ADMISSIBLE = 16
GROUP_LEAVES = 128
LEAVES = 1024
PARENTS = 512
N_GRP = 8
N_LEAF = 64


def draw_self_blocks(key, part):
    key = jax.random.fold_in(key, 11)
    noise_key = jax.random.fold_in(key, 0)
    dims = (LEAVES, LEAF_SIZE, LEAF_SIZE)
    noise_values = jax.random.normal(noise_key, dims, jnp.float32) * 0.02
    scales = jnp.ones((LEAVES, LEAF_SIZE), jnp.float32)
    mirrored = 0.5 * (noise_values + jnp.swapaxes(noise_values, 1, 2))
    identity = jnp.eye(LEAF_SIZE, dtype=jnp.float32)
    outside = mirrored * (1.0 - identity)
    dominance = jnp.sum(jnp.abs(outside), axis=2) + 0.25 * scales
    return (outside + identity * dominance[:, :, None]).astype(jnp.bfloat16)


def draw_near_list(key, part):
    key = jax.random.fold_in(key, 23)
    leaf_ids = jnp.arange(LEAVES, dtype=jnp.int32)
    device = leaf_ids // LEAF_DEV
    place = device % (GROUP_LEAVES // LEAF_DEV)
    final_place = GROUP_LEAVES // LEAF_DEV - 1
    upward = leaf_ids % 2 == 1
    upward = jnp.where(place == 0, True, jnp.where(place == final_place, False, upward))
    neighbour = jnp.where(upward, device + 1, device - 1)
    picks = jax.random.randint(key, (LEAVES, NEAR_LINKS), 0, LEAF_DEV, dtype=jnp.int32)
    return neighbour[:, None] * LEAF_DEV + picks


def block_levels(key, shape, cuts, low, top_value):
    factor_of = 1.0
    for position, shards_of in cuts:
        heights = jax.random.uniform(jax.random.fold_in(jax.random.fold_in(key, 6), position), (shards_of,), jnp.float32, low / len(cuts), top_value / len(cuts))
        factor_of = factor_of * jnp.repeat(jnp.exp(heights), shape[position] // shards_of).reshape((-1,) + (1,) * (len(shape) - 1 - position))
    return factor_of


def shared_out(key, own, number, rows, number_of, top, most, slope):
    sequence = jax.random.permutation(key, number_of)
    crowded, ordinary = load_shares(number_of, rows * top, most, slope, True), load_shares(number_of, rows * top, most, slope, False)
    places = jnp.arange(number_of)

    def named(lengths, offset_by):
        used = int((lengths > 0).sum())
        fixed = max(1, used // 4)
        passed = fixed + (places - fixed + offset_by * (used - fixed)) % max(1, number_of - fixed)
        return jnp.zeros((number_of,), jnp.int32).at[sequence[jnp.where(places < fixed, places, passed)]].set(jnp.asarray(lengths, jnp.int32))

    lengths = jnp.where(number % 4 == 0, named(crowded, number // 4), named(ordinary, number - number // 4 - 1))
    mixed = jax.random.permutation(jax.random.fold_in(own, 3), number_of)
    source_of, sink = mixed[0:number_of // 2 * 2:2], mixed[1:number_of // 2 * 2:2]
    margin = jnp.minimum(lengths[source_of] - 1, most - lengths[sink]) // 2
    margin = jnp.where((source_of == sequence[0]) | (sink == sequence[0]) | (lengths[sink] == 0), 0, jnp.maximum(margin, 0))
    passed = jax.random.randint(jax.random.fold_in(own, 4), (number_of // 2,), 0, 1 << 20) % (margin + 1)
    lengths = lengths.at[source_of].add(-passed).at[sink].add(passed)
    labels = jnp.searchsorted(jnp.cumsum(lengths), jnp.arange(rows * top), side="right").astype(jnp.int32)
    listing = labels.reshape(top, rows).T
    listing = listing[jax.random.permutation(jax.random.fold_in(own, 1), rows)]
    offset_by = jax.random.randint(jax.random.fold_in(own, 2), (rows, 1), 0, top)
    return jnp.take_along_axis(listing, (jnp.arange(top)[None, :] + offset_by) % top, axis=1)


def load_shares(number_of, total, reach, skew, full):
    loads = [(1 << 20) // math.isqrt(rank ** skew) + 1 for rank in range(1, number_of + 1)]
    largest = reach if full else min(reach, max(-(-total // number_of), total * loads[0] // sum(loads)))
    least = 1 if total - largest >= number_of - 1 else 0
    given, spare = [largest] + [least] * (number_of - 1), total - largest - least * (number_of - 1)
    while spare > 0:
        free = [i for i in range(1, number_of) if given[i] < largest] or [i for i in range(1, number_of) if given[i] < reach]
        whole, budget = sum([loads[i] for i in free]), spare
        for i in free:
            extra = min(reach - given[i], max(1, budget * loads[i] // whole), spare)
            given[i] = given[i] + extra
            spare = spare - extra
    return np.array(given)


def scatter_about(own_key, shape, scale, most, cuts=(), kind=jnp.bfloat16):
    drawn = jax.random.normal(own_key, shape, jnp.float32) * scale
    if len(cuts) > 0:
        drawn = block_levels(own_key, shape, cuts, -0.22, 0.18) * drawn
    return jnp.clip(drawn, min=-most, max=most).astype(kind)


def setup_inputs(seed: int = 0) -> dict:
    seeds = jax.random.split(jax.random.key(seed), 9)
    self_blocks = draw_self_blocks(jax.random.fold_in(seeds[8], 71), 0)
    near_blocks = scatter_about(seeds[1], (LEAVES, NEAR_LINKS, LEAF_SIZE, LEAF_SIZE), 1.0, 6.0, ((0, 512),))
    leaf_basis = scatter_about(seeds[2], (LEAVES, LEAF_SIZE, LEAF_SIZE), LEAF_SIZE ** -0.5, 0.25, ((0, 512),))
    transfer = scatter_about(seeds[3], (LEAVES, ADMISSIBLE, SKELETON, SKELETON), SKELETON ** -0.5, 0.5, ((0, 512),))
    near_list = draw_near_list(jax.random.fold_in(seeds[8], 71), 0)
    adm_list_keys = jax.random.split(jax.random.fold_in(seeds[5], 1), LEAVES // LEAF_DEV)
    adm_list_turns = jax.random.permutation(jax.random.fold_in(seeds[5], 3), LEAVES // LEAF_DEV)
    adm_list = jax.vmap(lambda own, number: shared_out(jax.random.fold_in(seeds[5], 2), own, number, LEAF_DEV, N_LEAF, ADMISSIBLE, LEAF_DEV, 2))(adm_list_keys, adm_list_turns).reshape((LEAVES, ADMISSIBLE))
    parent_kernel = scatter_about(seeds[6], (PARENTS, SKELETON, SKELETON), (SKELETON ** 3) ** -0.5, 0.00390625, ((0, 512),))
    chain_coupling = scatter_about(seeds[7], (N_GRP, SKELETON, SKELETON), SKELETON ** -0.5, 0.5, ((0, 8),), jnp.float32)
    return {"self_blocks": self_blocks, "near_blocks": near_blocks, "leaf_basis": leaf_basis, "transfer": transfer, "near_list": near_list, "adm_list": adm_list, "parent_kernel": parent_kernel, "chain_coupling": chain_coupling}


highest = lax.Precision.HIGHEST

def solve_block(factor, right_side):
    return jax.scipy.linalg.cho_solve((factor, True), right_side)

def eliminate(blocks, basis):
    projected = jnp.einsum('lbq,lbc->lqc', basis.astype(jnp.float32), blocks.astype(jnp.float32), precision=highest).astype(jnp.bfloat16)
    reduced = jnp.einsum('lqc,lcp->lqp', projected.astype(jnp.float32), basis.astype(jnp.float32), precision=highest)
    inner_block = reduced[:, :REDUNDANT, :REDUNDANT]
    upper_block = reduced[:, :REDUNDANT, REDUNDANT:]
    lower_block = reduced[:, REDUNDANT:, :REDUNDANT]
    corner = reduced[:, REDUNDANT:, REDUNDANT:]
    factor = jnp.linalg.cholesky(inner_block)
    solved = jax.vmap(solve_block)(factor, upper_block)
    return corner - jnp.einsum('lkr,lrm->lkm', lower_block, solved, precision=highest)

def group_work(inputs):
    blocks, near_blocks, basis, transfer, near_list, adm_list, kernels, first_leaf = inputs
    schur_block = eliminate(blocks, basis)
    skeleton = basis[:, :, REDUNDANT:]
    local_ids = (near_list - first_leaf).astype(jnp.int32).reshape(-1)
    partners = jnp.take(skeleton, local_ids, axis=0).reshape(GROUP_LEAVES, NEAR_LINKS, LEAF_SIZE, SKELETON)
    facing = jnp.einsum('lbk,ljbc->ljkc', skeleton.astype(jnp.float32), near_blocks.astype(jnp.float32), precision=highest).astype(jnp.bfloat16)
    coupling = jnp.einsum('ljkc,ljcm->lkm', facing.astype(jnp.float32), partners.astype(jnp.float32), precision=highest)
    lowered = schur_block.astype(jnp.bfloat16)
    lifted = jnp.einsum('lkm,lamn->lakn', lowered.astype(jnp.float32), transfer.astype(jnp.float32), precision=highest).astype(jnp.bfloat16)
    chosen = jnp.take(kernels, adm_list.reshape(-1).astype(jnp.int32), axis=0).reshape(GROUP_LEAVES, ADMISSIBLE, SKELETON, SKELETON)
    mixture = jnp.einsum('lakm,lame->lake', chosen.astype(jnp.float32), lifted.astype(jnp.float32), precision=highest).astype(jnp.bfloat16)
    item_terms = jnp.einsum('lamk,lame->lake', lifted.astype(jnp.float32), mixture.astype(jnp.float32), precision=highest)
    parent = jax.ops.segment_sum(item_terms.reshape(-1, SKELETON, SKELETON), adm_list.reshape(-1).astype(jnp.int32), num_segments=N_LEAF)
    return (schur_block + coupling, parent)

def reference(self_blocks, near_blocks, leaf_basis, transfer, near_list, adm_list, parent_kernel, chain_coupling):
    grouped = (self_blocks.reshape(N_GRP, GROUP_LEAVES, LEAF_SIZE, LEAF_SIZE), near_blocks.reshape(N_GRP, GROUP_LEAVES, NEAR_LINKS, LEAF_SIZE, LEAF_SIZE), leaf_basis.reshape(N_GRP, GROUP_LEAVES, LEAF_SIZE, LEAF_SIZE), transfer.reshape(N_GRP, GROUP_LEAVES, ADMISSIBLE, SKELETON, SKELETON), near_list.reshape(N_GRP, GROUP_LEAVES, NEAR_LINKS), adm_list.reshape(N_GRP, GROUP_LEAVES, ADMISSIBLE), parent_kernel.reshape(N_GRP, N_LEAF, SKELETON, SKELETON), jnp.arange(N_GRP, dtype=jnp.int32) * GROUP_LEAVES)
    leaf_out, parent_out = lax.map(group_work, grouped)
    group_roots = jnp.mean(parent_out, axis=1)
    identity = jnp.eye(SKELETON, dtype=jnp.float32)
    carried = jnp.zeros((SKELETON, SKELETON), jnp.float32)
    top_list = []
    for group_index in range(N_GRP):
        step_map = 0.8 * identity + 0.5 * chain_coupling[group_index]
        carried = jnp.dot(step_map.T, jnp.dot(carried, step_map, precision=highest), precision=highest) + group_roots[group_index]
        top_list.append(carried)
    return (leaf_out.reshape(LEAVES, SKELETON, SKELETON), parent_out.reshape(PARENTS, SKELETON, SKELETON), jnp.stack(top_list))
```

```python
import functools

import jax
import jax.numpy as jnp
from jax import lax
from jax.experimental import pallas as pl
from jax.experimental.pallas import tpu as pltpu
from jax.sharding import PartitionSpec as P

f32 = jnp.float32
bf16 = jnp.bfloat16
MESH = pl.DeviceIdType.MESH
VMEM = pl.BlockSpec(memory_space=pltpu.VMEM)
SMEM = pl.BlockSpec(memory_space=pltpu.SMEM)
ANY = pl.BlockSpec(memory_space=pl.ANY)
RING = 8
RANK = 128
HALF = 64
TILE = (8, 128)


def dot(a, b):
    return jnp.dot(a, b, preferred_element_type=f32)


def dot_t(a, b):
    return lax.dot_general(a, b, (((0,), (0,)), ((), ())), preferred_element_type=f32)


def dot_full(a, b):
    return jnp.dot(a, b, precision=lax.Precision.HIGHEST, preferred_element_type=f32)


def dot_t_full(a, b):
    return lax.dot_general(
        a, b, (((0,), (0,)), ((), ())), precision=lax.Precision.HIGHEST, preferred_element_type=f32
    )


def invert_pair(mats):
    lane = lax.broadcasted_iota(jnp.int32, TILE, 1)
    sub = lax.broadcasted_iota(jnp.int32, TILE, 0)
    lane_all = lax.broadcasted_iota(jnp.int32, (RANK, RANK), 1)
    steps = RANK // 8
    spread = lambda x: jnp.broadcast_to(x, TILE)
    ahead = [a[0:8] for a in mats]
    for s in range(steps):
        c0 = 8 * s
        inside = (lane >= c0) & (lane < c0 + 8)
        inside_all = (lane_all >= c0) & (lane_all < c0 + 8)
        last = s + 1 == steps
        strips, coming = [], []
        for a, strip in zip(mats, ahead):
            cols = [spread(strip[:, c0 + i : c0 + i + 1]) for i in range(8)]
            block = {(j, i): spread(cols[i][j : j + 1]) for i in range(8) for j in range(i, 8)}
            rows = [
                jnp.where(inside, jnp.where(lane == c0 + j, 1.0, 0.0), spread(strip[j : j + 1]))
                for j in range(8)
            ]
            if not last:
                below = a[c0 + 8 : c0 + 16]
                left = [spread(below[:, c0 + i : c0 + i + 1]) for i in range(8)]
                following = jnp.where(inside, 0.0, below)
            pivots, mult = [], {}
            for k in range(8):
                pivots.append(1.0 / block[k, k])
                for j in range(k + 1, 8):
                    for i in range(k + 1, j + 1):
                        block[j, i] = block[j, i] - (block[j, k] * block[i, k]) * pivots[k]
                    mult[j, k] = block[j, k] * pivots[k]
                for j in range(k + 1, 8):
                    rows[j] = rows[j] - mult[j, k] * rows[k]
                    if not last:
                        left[j] = left[j] - mult[j, k] * left[k]
                if not last:
                    following = following - left[k] * (rows[k] * pivots[k])
            if not last:
                coming.append(following)
            rows = [rows[k] * pivots[k] for k in range(8)]
            for k in range(7, 0, -1):
                for j in range(k):
                    rows[j] = rows[j] - mult[k, j] * rows[k]
            strip = rows[0]
            for j in range(1, 8):
                strip = jnp.where(sub == j, rows[j], strip)
            strips.append(strip)
        results = []
        for a, strip in zip(mats, strips):
            nothing = jnp.zeros_like(strip)
            placed = jnp.concatenate([strip if t == s else nothing for t in range(steps)], axis=0)
            a = jnp.where(inside_all, 0.0, a) - dot_full(a, placed)
            results.append(
                jnp.concatenate([strip if t == s else a[8 * t : 8 * t + 8] for t in range(steps)], axis=0)
            )
        mats, ahead = results, coming
    return mats


def form_reduced(leaves, blocks_ref, basis_ref, reduced):
    parts = basis_ref.shape[1] // RANK
    for l in range(leaves):
        basis = basis_ref[l]
        turned = dot(blocks_ref[l], basis).astype(bf16)
        reduced[l] = dot_t(turned, basis)
        for i in range(parts - 1):
            for j in range(i, parts - 1):
                si, sj = pl.ds(RANK * i, RANK), pl.ds(RANK * j, RANK)
                x = 0.5 * (reduced[l, si, sj] + reduced[l, sj, si].T)
                reduced[l, si, sj] = x
                if j > i:
                    reduced[l, sj, si] = x.T


def eliminate_block(leaves, k, parts, reduced):
    here = pl.ds(RANK * k, RANK)
    rest = pl.ds(RANK * (k + 1), RANK * (parts - 1 - k))
    inverses = invert_pair([reduced[l, here, here] for l in range(leaves)])
    for l in range(leaves):
        solved = dot_full(inverses[l], reduced[l, here, rest])
        reduced[l, rest, rest] = reduced[l, rest, rest] - dot_full(reduced[l, rest, here], solved)


def schur_kernel(near_list, blocks_ref, basis_ref, near_ref, halo, schur_ref, panels_ref, reduced):
    leaves, width = blocks_ref.shape[:2]
    parts = width // RANK
    skeleton = pl.ds(width - RANK, RANK)
    form_reduced(leaves, blocks_ref, basis_ref, reduced)
    for k in range(parts - 1):
        eliminate_block(leaves, k, parts, reduced)
    first = ((lax.axis_index("grp") * lax.axis_size("leaf") + lax.axis_index("leaf")) - 1) * leaves
    for l in range(leaves):
        schur = reduced[l, skeleton, skeleton]
        schur_ref[l] = schur
        place = near_list[l, 0] - first
        place = jnp.where(place < leaves, place, place - leaves)
        facing = dot_t(basis_ref[l, :, skeleton], near_ref[l, 0]).astype(bf16)
        panels_ref[l] = schur + dot(facing, halo[place])


class Places:
    def __init__(self):
        self.grp = lax.axis_index("grp")
        self.leaf = lax.axis_index("leaf")
        self.z = self.leaf // RING
        self.y = self.leaf % RING

    def on_z(self, z):
        return (self.grp, z * RING + self.y)

    def on_y(self, y):
        return (self.grp, self.z * RING + y)

    def on_grp(self, grp):
        return (grp, self.leaf)

    def on_leaf(self, step):
        n = lax.axis_size("leaf")
        return (self.grp, (self.leaf + step + n) % n)


def others(pos):
    return [(pos + o) % RING for o in range(1, RING)]


def greet(at, leaf_line):
    barrier = pltpu.get_barrier_semaphore()
    ids = [at.on_z(i) for i in others(at.z)] + [at.on_y(i) for i in others(at.y)]
    ids += [at.on_grp(i) for i in others(at.grp)]
    if leaf_line:
        ids += [at.on_leaf(1), at.on_leaf(-1)]
    for i in ids:
        pl.semaphore_signal(barrier, inc=1, device_id=i, device_id_type=MESH)
    pl.semaphore_wait(barrier, len(ids))


def remote(src, dst, send, recv, to):
    return pltpu.make_async_remote_copy(
        src_ref=src, dst_ref=dst, send_sem=send, recv_sem=recv, device_id=to, device_id_type=MESH
    )


def exchange(pos, to, src, dst, send, recv):
    copies = []
    for o in range(1, RING):
        i = (pos + o) % RING
        copy = remote(src(i), dst.at[pos], send.at[o], recv.at[o], to(i))
        copy.start()
        copies.append(copy)
    return copies


def wait_all(copies):
    for copy in copies:
        copy.wait()


def spread_kernel(kernel_ref, basis_ref, chain_ref, upper, lower, halo, chain, send_1, recv_1, send_2, recv_2, own):
    at = Places()
    leaves, width = basis_ref.shape[:2]
    skeleton = basis_ref.at[:, :, pl.ds(width - RANK, RANK)]
    top = kernel_ref.at[0, pl.ds(0, HALF)]
    bottom = kernel_ref.at[0, pl.ds(HALF, HALF)]
    mine = [
        pltpu.make_async_copy(top, upper.at[at.y, at.z], own.at[0]),
        pltpu.make_async_copy(bottom, lower.at[at.z, at.y], own.at[1]),
        pltpu.make_async_copy(chain_ref.at[0], chain.at[at.grp], own.at[2]),
    ]
    for copy in mine:
        copy.start()
    greet(at, True)
    first = exchange(at.z, at.on_z, lambda i: top, upper.at[at.y], send_1.at[0], recv_1.at[0])
    second = exchange(at.y, at.on_y, lambda i: bottom, lower.at[at.z], send_1.at[1], recv_1.at[1])
    third = exchange(at.grp, at.on_grp, lambda i: chain_ref.at[0], chain, send_1.at[2], recv_1.at[2])
    to_right = remote(skeleton, halo.at[pl.ds(0, leaves)], send_1.at[0, 0], recv_1.at[0, 0], at.on_leaf(1))
    to_left = remote(skeleton, halo.at[pl.ds(leaves, leaves)], send_1.at[1, 0], recv_1.at[1, 0], at.on_leaf(-1))
    to_right.start()
    to_left.start()
    wait_all(mine)
    wait_all(first)
    wait_all(second)
    for t in range(1, RING // 2 + 1):
        copies = []
        for h, (table, pos, to) in enumerate(((upper, at.y, at.on_y), (lower, at.z, at.on_z))):
            up = (pos - t + 1 + RING) % RING
            copies.append(remote(table.at[up], table.at[up], send_2.at[h, 0, t], recv_2.at[h, 0, t], to((pos + 1) % RING)))
            if t < RING // 2:
                down = (pos + t - 1) % RING
                copies.append(
                    remote(table.at[down], table.at[down], send_2.at[h, 1, t], recv_2.at[h, 1, t], to((pos + RING - 1) % RING))
                )
        for copy in copies:
            copy.start()
        wait_all(copies)
    wait_all(third)
    to_right.wait()
    to_left.wait()


def merge_kernel(
    adm, inverse, schur_ref, transfer_ref, upper, lower, chain_ref, parent_ref, top_ref,
    terms, shares, down_in, up_in, near_sum, far_in, local, slabs, slab_in, prefix, cross,
    send_c, recv_c, send_f, recv_f, send_r, recv_r,
):
    at = Places()
    leaves, entries = transfer_ref.shape[:2]
    greet(at, False)

    local[...] = jnp.zeros_like(local)
    lowered = [schur_ref[l].astype(bf16) for l in range(leaves)]

    for l in range(leaves):

        @pl.loop(0, entries // 4)
        def _(step, l=l):
            total = local[...]
            for i in range(4):
                a = step * 4 + i
                p = adm[l, a]
                pz, py = p // RING, p % RING
                lifted = dot(lowered[l], transfer_ref[l, a]).astype(bf16)
                kernel = jnp.concatenate([upper[py, pz], lower[pz, py]], axis=0)
                mixture = dot(kernel, lifted).astype(bf16)
                term = dot_t(lifted, mixture)
                terms[l * entries + a] = term.astype(bf16)
                total = total + term
            local[...] = total

    terms[leaves * entries] = jnp.zeros((RANK, RANK), bf16)

    @pl.loop(0, RING)
    def _(pz):
        for py in range(RING):
            p = pz * RING + py
            share = terms[inverse[0, p]].astype(f32)
            for l in range(1, leaves):
                share = share + terms[inverse[l, p]].astype(f32)
            share = share.astype(bf16)
            shares[0, pz, py] = share[:HALF]
            shares[1, py, pz] = share[HALF:]

    lines = ((at.z, at.on_z), (at.y, at.on_y))
    size = RING // 2

    def down_copy(h, t):
        pos, to = lines[h]
        src = shares.at[h, (pos - 5 + t + RING) % RING] if t == 1 else down_in.at[h, t - 2]
        return remote(src, down_in.at[h, t - 1], send_c.at[h, 0, t], recv_c.at[h, 0, t], to((pos + RING - 1) % RING))

    def up_copy(h, t):
        pos, to = lines[h]
        src = shares.at[h, (pos + 4 - t) % RING] if t == 1 else up_in.at[h, t - 2]
        return remote(src, up_in.at[h, t - 1], send_c.at[h, 1, t], recv_c.at[h, 1, t], to((pos + 1) % RING))

    def add_share(buffer, h, chunk):
        @pl.loop(0, RING)
        def _(i):
            buffer[i] = (buffer[i].astype(f32) + shares[h, chunk, i].astype(f32)).astype(bf16)

    down = [[None] * (size + 1) for _ in range(2)]
    up = [[None] * (size + 1) for _ in range(2)]
    for h in range(2):
        down[h][1] = down_copy(h, 1)
        down[h][1].start()
        up[h][1] = up_copy(h, 1)
        up[h][1].start()

    depth = RANK // RING
    r1 = exchange(
        at.z, at.on_z, lambda i: local.at[pl.ds(pl.multiple_of(i * depth, depth), depth)], slab_in.at[0],
        send_r.at[0], recv_r.at[0],
    )

    eye = (
        lax.broadcasted_iota(jnp.int32, (RANK, RANK), 0) == lax.broadcasted_iota(jnp.int32, (RANK, RANK), 1)
    ).astype(f32)
    running = jnp.zeros((RANK, RANK), f32)
    for j in range(RING - 1, -1, -1):
        if j < RING - 1:
            step_map = 0.8 * eye + 0.5 * chain_ref[j + 1]
            running = jnp.where(j < at.grp, dot_full(step_map, running), 0.0)
        running = jnp.where(j == at.grp, eye, running)
        prefix[j] = running

    def chain_step(t):
        for h in range(2):
            pos, _ = lines[h]
            down[h][t - 1].wait()
            add_share(down_in.at[h, t - 2], h, (pos - 5 + t + RING) % RING)
            down[h][t] = down_copy(h, t)
            down[h][t].start()
            up[h][t - 1].wait()
            if t < size:
                add_share(up_in.at[h, t - 2], h, (pos + 4 - t) % RING)
                up[h][t] = up_copy(h, t)
                up[h][t].start()

    def gathered(stage, pos, mine):
        total = mine
        for o in range(1, RING):
            total = total + slab_in[stage, (pos + o) % RING]
        return total

    chain_step(2)
    wait_all(r1)
    slabs[0] = gathered(0, at.z, local[pl.ds(pl.multiple_of(at.z * depth, depth), depth)])
    r2 = exchange(at.y, at.on_y, lambda i: slabs.at[0], slab_in.at[1], send_r.at[1], recv_r.at[1])
    chain_step(3)
    wait_all(r2)
    slabs[1] = gathered(1, at.y, slabs[0]) * (1.0 / (RING * RING))
    r3 = exchange(at.grp, at.on_grp, lambda i: slabs.at[1], slab_in.at[2], send_r.at[2], recv_r.at[2])
    chain_step(4)
    wait_all(r3)
    slab_in[2, at.grp] = slabs[1]
    mine = pl.ds(pl.multiple_of(at.z * depth, depth), depth)
    rows = jnp.concatenate([prefix[j, mine] for j in range(RING)], axis=0)
    mapped = jnp.concatenate([dot_full(slab_in[2, j], prefix[j]) for j in range(RING)], axis=0)
    cross[...] = dot_t_full(rows, mapped)
    my_rows = pl.ds(pl.multiple_of(at.y * depth, depth), depth)
    r4 = exchange(at.z, at.on_z, lambda i: cross.at[my_rows], slab_in.at[3], send_r.at[3], recv_r.at[3])

    far = []
    for h in range(2):
        pos, _ = lines[h]
        down[h][size].wait()

        @pl.loop(0, RING)
        def _(i, h=h, pos=pos):
            near_sum[h, i] = (
                down_in[h, size - 1, i].astype(f32) + up_in[h, size - 2, i].astype(f32) + shares[h, pos, i].astype(f32)
            ).astype(bf16)

        other, to = lines[1 - h]
        far += exchange(other, to, lambda i, h=h: near_sum.at[h, i], far_in.at[h], send_f.at[h], recv_f.at[h])
    wait_all(r4)
    slabs[2] = gathered(3, at.z, cross[my_rows])
    r5 = exchange(at.y, at.on_y, lambda i: slabs.at[2], slab_in.at[4], send_r.at[4], recv_r.at[4])
    wait_all(far)
    for h in range(2):
        other, _ = lines[1 - h]
        total = near_sum[h, other].astype(f32)
        for o in range(1, RING):
            total = total + far_in[h, (other + o) % RING].astype(f32)
        parent_ref[0, pl.ds(h * HALF, HALF)] = total
    wait_all(r5)
    slab_in[4, at.y] = slabs[2]
    for i in range(RING):
        top_ref[0, pl.ds(i * depth, depth)] = slab_in[4, i]


def per_device(self_blocks, near_blocks, leaf_basis, transfer, near_list, adm_list, parent_kernel, chain_coupling):
    leaves, width = leaf_basis.shape[:2]
    entries = transfer.shape[1]
    depth = RANK // RING
    sems = pltpu.SemaphoreType.DMA
    shape = jax.ShapeDtypeStruct
    upper, lower, halo, chain = pl.pallas_call(
        spread_kernel,
        out_shape=(
            shape((RING, RING, HALF, RANK), bf16),
            shape((RING, RING, HALF, RANK), bf16),
            shape((2 * leaves, width, RANK), bf16),
            shape((RING, RANK, RANK), f32),
        ),
        in_specs=[ANY, ANY, ANY],
        out_specs=(ANY, ANY, ANY, ANY),
        scratch_shapes=[
            sems((3, RING)), sems((3, RING)), sems((2, 2, RING)), sems((2, 2, RING)), sems((3,)),
        ],
        compiler_params=pltpu.CompilerParams(collective_id=0, has_side_effects=True),
    )(parent_kernel, leaf_basis, chain_coupling)
    schur, panels = pl.pallas_call(
        schur_kernel,
        out_shape=(shape((leaves, RANK, RANK), f32), shape((leaves, RANK, RANK), f32)),
        in_specs=[SMEM, VMEM, VMEM, VMEM, VMEM],
        out_specs=(VMEM, VMEM),
        scratch_shapes=[pltpu.VMEM((leaves, width, width), f32)],
        compiler_params=pltpu.CompilerParams(vmem_limit_bytes=40 * 2**20),
    )(near_list, self_blocks, leaf_basis, near_blocks, halo)
    order = jnp.arange(leaves * entries, dtype=jnp.int32).reshape(leaves, entries, 1)
    names = adm_list[:, :, None] == jnp.arange(RING * RING, dtype=jnp.int32)[None, None, :]
    inverse = jnp.min(jnp.where(names, order, leaves * entries), axis=1)
    parent, top = pl.pallas_call(
        merge_kernel,
        out_shape=(shape((1, RANK, RANK), f32), shape((1, RANK, RANK), f32)),
        in_specs=[SMEM, SMEM, VMEM, VMEM, VMEM, VMEM, VMEM],
        out_specs=(VMEM, VMEM),
        scratch_shapes=[
            pltpu.VMEM((leaves * entries + 1, RANK, RANK), bf16),
            pltpu.VMEM((2, RING, RING, HALF, RANK), bf16),
            pltpu.VMEM((2, RING // 2, RING, HALF, RANK), bf16),
            pltpu.VMEM((2, RING // 2 - 1, RING, HALF, RANK), bf16),
            pltpu.VMEM((2, RING, HALF, RANK), bf16),
            pltpu.VMEM((2, RING, HALF, RANK), bf16),
            pltpu.VMEM((RANK, RANK), f32),
            pltpu.VMEM((3, depth, RANK), f32),
            pltpu.VMEM((5, RING, depth, RANK), f32),
            pltpu.VMEM((RING, RANK, RANK), f32),
            pltpu.VMEM((RANK, RANK), f32),
            sems((2, 2, RING)), sems((2, 2, RING)),
            sems((2, RING)), sems((2, RING)),
            sems((5, RING)), sems((5, RING)),
        ],
        compiler_params=pltpu.CompilerParams(
            collective_id=1, has_side_effects=True, vmem_limit_bytes=40 * 2**20
        ),
    )(adm_list, inverse, schur, transfer, upper, lower, chain)
    return panels, parent, top


def solution(mesh):
    lead = P(("grp", "leaf"))
    return jax.shard_map(
        per_device,
        mesh=mesh,
        in_specs=(lead, lead, lead, lead, lead, lead, lead, P("grp")),
        out_specs=(lead, lead, P("grp")),
        check_vma=False,
    )
```

```python
import functools

import jax
import jax.numpy as jnp
from jax import lax
from jax.experimental import pallas as pl
from jax.experimental.pallas import tpu as pltpu
from jax.sharding import PartitionSpec as P

f32 = jnp.float32
bf16 = jnp.bfloat16
MESH = pl.DeviceIdType.MESH
VMEM = pl.BlockSpec(memory_space=pltpu.VMEM)
SMEM = pl.BlockSpec(memory_space=pltpu.SMEM)
ANY = pl.BlockSpec(memory_space=pl.ANY)
RING = 8
RANK = 128
HALF = 64
TILE = (8, 128)


def dot(a, b):
    return jnp.dot(a, b, preferred_element_type=f32)


def dot_t(a, b):
    return lax.dot_general(a, b, (((0,), (0,)), ((), ())), preferred_element_type=f32)


def dot_full(a, b):
    return jnp.dot(a, b, precision=lax.Precision.HIGHEST, preferred_element_type=f32)


def dot_t_full(a, b):
    return lax.dot_general(
        a, b, (((0,), (0,)), ((), ())), precision=lax.Precision.HIGHEST, preferred_element_type=f32
    )


def factor_strip(strip, below, c0):
    shape = strip.shape
    lane = lax.broadcasted_iota(jnp.int32, shape, 2)
    sub = lax.broadcasted_iota(jnp.int32, shape, 1)
    inside = (lane >= c0) & (lane < c0 + 8)
    column = lambda x, i: jnp.broadcast_to(x[:, :, c0 + i : c0 + i + 1], shape)
    row = lambda x, j: jnp.broadcast_to(x[:, j : j + 1], shape)
    columns = [column(strip, i) for i in range(8)]
    block = [jnp.stack([row(columns[i], j) for j in range(i, 8)], axis=0) for i in range(8)]
    rows = jnp.stack(
        [jnp.where(inside, jnp.where(lane == c0 + j, 1.0, 0.0), row(strip, j)) for j in range(8)], axis=0
    )
    following = None
    if below is not None:
        left = jnp.stack([column(below, i) for i in range(8)], axis=0)
        following = jnp.where(inside, 0.0, below)
    mult, scaled = [], []
    for k in range(8):
        pivot = 1.0 / block[k][0]
        for i in range(k + 1, 8):
            block[i] = block[i] - (block[k][i - k :] * block[k][i - k]) * pivot
        scaled.append(rows[0] * pivot)
        if below is not None:
            following = following - left[0] * scaled[k]
        if k < 7:
            mult.append(block[k][1:] * pivot)
            rows = rows[1:] - mult[k] * rows[0]
            if below is not None:
                left = left[1:] - mult[k] * left[0]
    rows = jnp.stack(scaled, axis=0)
    result = None
    for k in range(7, -1, -1):
        result = rows[k] if result is None else jnp.where(sub == k, rows[k], result)
        if k > 0:
            rows = rows[:k] - jnp.stack([mult[j][k - j - 1] for j in range(k)], axis=0) * rows[k]
    return result, following


def invert(mats, between):
    leaves = mats.shape[0]
    lane = lax.broadcasted_iota(jnp.int32, (RANK, RANK), 1)
    steps = RANK // 8
    ahead = mats[:, 0:8]
    for s in range(steps):
        c0 = 8 * s
        strip, ahead = factor_strip(ahead, mats[:, c0 + 8 : c0 + 16] if s + 1 < steps else None, c0)
        inside = (lane >= c0) & (lane < c0 + 8)
        results = []
        for l in range(leaves):
            nothing = jnp.zeros(TILE, f32)
            placed = jnp.concatenate([strip[l] if t == s else nothing for t in range(steps)], axis=0)
            rest = jnp.where(inside, 0.0, mats[l]) - dot_full(mats[l], placed)
            results.append(
                jnp.concatenate([strip[l] if t == s else rest[8 * t : 8 * t + 8] for t in range(steps)], axis=0)
            )
        mats = jnp.stack(results, axis=0)
        between(s)
    return mats


def form_reduced(l, parts, blocks, basis, reduced):
    turned = dot(blocks[l], basis[l]).astype(bf16)
    reduced[l] = dot_t(turned, basis[l])
    for i in range(parts - 1):
        for j in range(i, parts - 1):
            si, sj = pl.ds(RANK * i, RANK), pl.ds(RANK * j, RANK)
            x = 0.5 * (reduced[l, si, sj] + reduced[l, sj, si].T)
            reduced[l, si, sj] = x
            if j > i:
                reduced[l, sj, si] = x.T


def eliminate(leaves, parts, reduced, inverses, between):
    @pl.loop(0, parts - 1)
    def _(k):
        here = pl.ds(pl.multiple_of(k * RANK, RANK), RANK)
        inverses[...] = invert(reduced[:, here, here], functools.partial(between, k))
        for known in range(parts - 1):

            @pl.when(k == known)
            def _(known=known):
                here = pl.ds(RANK * known, RANK)
                rest = pl.ds(RANK * (known + 1), RANK * (parts - 1 - known))
                for l in range(leaves):
                    solved = dot_full(inverses[l], reduced[l, here, rest])
                    reduced[l, rest, rest] = reduced[l, rest, rest] - dot_full(reduced[l, rest, here], solved)


class Places:
    def __init__(self):
        self.grp = lax.axis_index("grp")
        self.leaf = lax.axis_index("leaf")
        self.z = self.leaf // RING
        self.y = self.leaf % RING

    def on_z(self, z):
        return (self.grp, z * RING + self.y)

    def on_y(self, y):
        return (self.grp, self.z * RING + y)

    def on_grp(self, grp):
        return (grp, self.leaf)

    def on_leaf(self, step):
        n = lax.axis_size("leaf")
        return (self.grp, (self.leaf + step + n) % n)


def others(pos):
    return [(pos + o) % RING for o in range(1, RING)]


def partners(at):
    ids = [at.on_z(i) for i in others(at.z)] + [at.on_y(i) for i in others(at.y)]
    return ids + [at.on_grp(i) for i in others(at.grp)] + [at.on_leaf(1), at.on_leaf(-1)]


def greet(at):
    for i in partners(at):
        pl.semaphore_signal(pltpu.get_barrier_semaphore(), inc=1, device_id=i, device_id_type=MESH)


def await_greetings(at):
    pl.semaphore_wait(pltpu.get_barrier_semaphore(), len(partners(at)))


def remote(src, dst, send, recv, to):
    return pltpu.make_async_remote_copy(
        src_ref=src, dst_ref=dst, send_sem=send, recv_sem=recv, device_id=to, device_id_type=MESH
    )


def exchange(pos, to, src, dst, send, recv):
    copies = []
    for o in range(1, RING):
        i = (pos + o) % RING
        copy = remote(src(i), dst.at[pos], send.at[o], recv.at[o], to(i))
        copy.start()
        copies.append(copy)
    return copies


def wait_all(copies):
    for copy in copies:
        copy.wait()


SIZE = RING // 2
PIECES = 2
DEPTH = RANK // RING
GATHER_AT = {(0, 3): 1, (0, 15): 2, (1, 13): 3, (2, 9): 4}


def kernel_body(
    near_list, adm, inverse, blocks_hbm, near_hbm, basis_hbm, transfer_hbm, kernel_hbm, chain_hbm,
    panels_ref, parent_ref, top_ref,
    blocks, near, basis, transfer, upper, lower, halo, maps, reduced, inverses, lifted, terms, shares,
    down_in, up_in, near_sum, far_in, local, local_in, prefix, cross, slabs, slab_in,
    load_sem, send_1, recv_1, send_2, recv_2, send_c, recv_c, send_f, recv_f, send_g, recv_g, send_r, recv_r,
):
    at = Places()
    leaves, width = basis.shape[:2]
    entries = transfer.shape[1]
    parts = width // RANK
    skeleton = pl.ds(width - RANK, RANK)
    lines = ((at.z, at.on_z), (at.y, at.on_y))

    top = kernel_hbm.at[0, pl.ds(0, HALF)]
    bottom = kernel_hbm.at[0, pl.ds(HALF, HALF)]
    loads = []
    for l in range(leaves):
        loads += [(basis_hbm.at[l], basis.at[l]), (blocks_hbm.at[l], blocks.at[l])]
    loads += [(near_hbm, near), (transfer_hbm, transfer)]
    loads += [(top, upper.at[at.y, at.z]), (bottom, lower.at[at.z, at.y]), (chain_hbm.at[0], maps.at[at.grp])]
    loads = [pltpu.make_async_copy(src, dst, load_sem.at[i]) for i, (src, dst) in enumerate(loads)]
    for load in loads:
        load.start()
    greet(at)

    for l in range(leaves):
        loads[2 * l].wait()
        loads[2 * l + 1].wait()
        form_reduced(l, parts, blocks, basis, reduced)
        if l == 0:
            await_greetings(at)
            exchange(at.z, at.on_z, lambda i: top, upper.at[at.y], send_1.at[0], recv_1.at[0])
            exchange(at.y, at.on_y, lambda i: bottom, lower.at[at.z], send_1.at[1], recv_1.at[1])
            exchange(at.grp, at.on_grp, lambda i: chain_hbm.at[0], maps, send_1.at[2], recv_1.at[2])

    def gather_copies(t):
        copies = []
        for h, (table, pos, to) in enumerate(((upper, at.y, at.on_y), (lower, at.z, at.on_z))):
            chunk = (pos - t + 1 + RING) % RING
            copies.append(
                remote(table.at[chunk], table.at[chunk], send_2.at[h, 0, t], recv_2.at[h, 0, t], to((pos + 1) % RING))
            )
            if t < SIZE:
                chunk = (pos + t - 1) % RING
                copies.append(
                    remote(
                        table.at[chunk], table.at[chunk], send_2.at[h, 1, t], recv_2.at[h, 1, t],
                        to((pos + RING - 1) % RING),
                    )
                )
        return copies

    def halo_copies():
        source = basis.at[:, :, skeleton]
        return [
            remote(source, halo.at[pl.ds(0, leaves)], send_1.at[0, 0], recv_1.at[0, 0], at.on_leaf(1)),
            remote(source, halo.at[pl.ds(leaves, leaves)], send_1.at[1, 0], recv_1.at[1, 0], at.on_leaf(-1)),
        ]

    def first_copies():
        return [
            remote(top, upper.at[at.y, at.z], send_1.at[0, o], recv_1.at[0, o], at.on_z((at.z + o) % RING))
            for o in range(1, RING)
        ] + [
            remote(bottom, lower.at[at.z, at.y], send_1.at[1, o], recv_1.at[1, o], at.on_y((at.y + o) % RING))
            for o in range(1, RING)
        ]

    def between(k, s):
        for (block, step), t in GATHER_AT.items():
            if s == step:

                @pl.when(k == block)
                def _(t=t):
                    if t == 1:
                        loads[-3].wait()
                        loads[-2].wait()
                        wait_all(first_copies())
                    else:
                        wait_all(gather_copies(t - 1))
                    for copy in gather_copies(t):
                        copy.start()
                    if t == SIZE:
                        for copy in halo_copies():
                            copy.start()

    eliminate(leaves, parts, reduced, inverses, between)

    loads[2 * leaves + 1].wait()
    group = 8
    for l in range(leaves):
        lowered = reduced[l, skeleton, skeleton].astype(bf16)

        @pl.loop(0, entries // group)
        def _(step, l=l, lowered=lowered):
            for i in range(group):
                a = step * group + i
                lifted[l * entries + a] = dot(lowered, transfer[l, a]).astype(bf16)

    wait_all(gather_copies(SIZE))
    local[...] = jnp.zeros_like(local)

    for l in range(leaves):

        @pl.loop(0, entries // group)
        def _(step, l=l):
            total = None
            for i in range(group):
                a = step * group + i
                p = adm[l, a]
                pz, py = p // RING, p % RING
                panel = lifted[l * entries + a]
                kernel = jnp.concatenate([upper[py, pz], lower[pz, py]], axis=0)
                mixture = dot(kernel, panel).astype(bf16)
                term = dot_t(panel, mixture)
                terms[l * entries + a] = term.astype(bf16)
                total = term if total is None else total + term
            local[...] += total

    terms[leaves * entries] = jnp.zeros((RANK, RANK), bf16)
    local_in[at.grp] = local[...].astype(bf16)
    by_grp = exchange(at.grp, at.on_grp, lambda i: local_in.at[at.grp], local_in, send_g, recv_g)

    @pl.loop(0, RING)
    def _(pz):
        for py in range(RING):
            p = pz * RING + py
            share = terms[inverse[0, p]].astype(f32)
            for l in range(1, leaves):
                share = share + terms[inverse[l, p]].astype(f32)
            share = share.astype(bf16)
            shares[0, pz, py] = share[:HALF]
            shares[1, py, pz] = share[HALF:]

    span = RING // PIECES

    def chain_copy(h, up, t, u):
        pos, to = lines[h]
        piece = pl.ds(u * span, span)
        buffer = (down_in, up_in)[up]
        chunk = (pos + 4 - t + RING) % RING if up else (pos - 5 + t + RING) % RING
        src = shares.at[h, chunk, piece] if t == 1 else buffer.at[h, t - 2, piece]
        target = (pos + 1) % RING if up else (pos + RING - 1) % RING
        return remote(src, buffer.at[h, t - 1, piece], send_c.at[h, up, t, u], recv_c.at[h, up, t, u], to(target))

    def chain_step(t):
        for u in range(PIECES):
            for h in range(2):
                pos, _ = lines[h]
                for up in range(2):
                    if t > 1:
                        chain_copy(h, up, t - 1, u).wait_recv()
                    if up and t == SIZE:
                        continue
                    if t > 1:
                        piece = pl.ds(u * span, span)
                        buffer = (down_in, up_in)[up]
                        chunk = (pos + 4 - t + RING) % RING if up else (pos - 5 + t + RING) % RING
                        mine = shares[h, chunk, piece].astype(f32)
                        buffer[h, t - 2, piece] = (buffer[h, t - 2, piece].astype(f32) + mine).astype(bf16)
                    chain_copy(h, up, t, u).start()

    chain_step(1)

    wait_all(
        [
            remote(chain_hbm.at[0], maps.at[at.grp], send_1.at[2, o], recv_1.at[2, o], at.on_grp((at.grp + o) % RING))
            for o in range(1, RING)
        ]
    )
    loads[-1].wait()
    eye = (
        lax.broadcasted_iota(jnp.int32, (RANK, RANK), 0) == lax.broadcasted_iota(jnp.int32, (RANK, RANK), 1)
    ).astype(f32)
    running = jnp.zeros((RANK, RANK), f32)
    for j in range(RING - 1, -1, -1):
        if j < RING - 1:
            step_map = 0.8 * eye + 0.5 * maps[j + 1]
            running = jnp.where(j < at.grp, dot_full(step_map, running), 0.0)
        running = jnp.where(j == at.grp, eye, running)
        high = running.astype(bf16)
        prefix[0, pl.ds(j * RANK, RANK)] = high
        prefix[1, pl.ds(j * RANK, RANK)] = (running - high.astype(f32)).astype(bf16)

    chain_step(2)

    wait_all(by_grp)
    mapped = jnp.concatenate(
        [
            dot(local_in[j], prefix[0, pl.ds(j * RANK, RANK)]) + dot(local_in[j], prefix[1, pl.ds(j * RANK, RANK)])
            for j in range(RING)
        ],
        axis=0,
    )
    high = mapped.astype(bf16)
    low = (mapped - high.astype(f32)).astype(bf16)
    cross[...] = (dot_t(prefix[0], high) + (dot_t(prefix[1], high) + dot_t(prefix[0], low))) * (1.0 / (RING * RING))

    slab = lambda i: pl.ds(pl.multiple_of(i * DEPTH, DEPTH), DEPTH)

    def gathered(stage, pos, mine):
        total = mine
        for o in range(1, RING):
            total = total + slab_in[stage, (pos + o) % RING]
        return total

    by_z = exchange(at.z, at.on_z, lambda i: cross.at[slab(i)], slab_in.at[0], send_r.at[0], recv_r.at[0])

    for copy in halo_copies():
        copy.wait()
    loads[2 * leaves].wait()
    first = ((at.grp * lax.axis_size("leaf") + at.leaf) - 1) * leaves
    for l in range(leaves):
        place = near_list[l, 0] - first
        place = jnp.clip(jnp.where(place < leaves, place, place - leaves), 0, 2 * leaves - 1)
        facing = dot_t(basis[l, :, skeleton], near[l, 0]).astype(bf16)
        panels_ref[l] = reduced[l, skeleton, skeleton] + dot(facing, halo[place])

    chain_step(3)
    wait_all(by_z)
    slabs[0] = gathered(0, at.z, cross[slab(at.z)])
    by_y = exchange(at.y, at.on_y, lambda i: slabs.at[0], slab_in.at[1], send_r.at[1], recv_r.at[1])
    chain_step(4)
    wait_all(by_y)
    slabs[1] = gathered(1, at.y, slabs[0])
    again = exchange(at.z, at.on_z, lambda i: slabs.at[1], slab_in.at[2], send_r.at[2], recv_r.at[2])

    far = []
    for h in range(2):
        pos, _ = lines[h]
        for u in range(PIECES):
            chain_copy(h, 0, SIZE, u).wait_recv()
        near_sum[h] = (
            down_in[h, SIZE - 1].astype(f32) + up_in[h, SIZE - 2].astype(f32) + shares[h, pos].astype(f32)
        ).astype(bf16)
        other, to = lines[1 - h]
        far += exchange(other, to, lambda i, h=h: near_sum.at[h, i], far_in.at[h], send_f.at[h], recv_f.at[h])
    wait_all(again)
    slab_in[2, at.z] = slabs[1]
    for i in range(RING):
        top_ref[0, pl.ds(i * DEPTH, DEPTH)] = slab_in[2, i]
    for h in range(2):
        for up in range(2):
            for t in range(1, SIZE + 1 - up):
                for u in range(PIECES):
                    chain_copy(h, up, t, u).wait_send()
    wait_all(far)
    for h in range(2):
        other, _ = lines[1 - h]
        total = near_sum[h, other].astype(f32)
        for o in range(1, RING):
            total = total + far_in[h, (other + o) % RING].astype(f32)
        parent_ref[0, pl.ds(h * HALF, HALF)] = total


def per_device(self_blocks, near_blocks, leaf_basis, transfer, near_list, adm_list, parent_kernel, chain_coupling):
    leaves, width = leaf_basis.shape[:2]
    entries = transfer.shape[1]
    order = jnp.arange(leaves * entries, dtype=jnp.int32).reshape(leaves, entries, 1)
    names = adm_list[:, :, None] == jnp.arange(RING * RING, dtype=jnp.int32)[None, None, :]
    inverse = jnp.min(jnp.where(names, order, leaves * entries), axis=1)
    sems = pltpu.SemaphoreType.DMA
    panel = jax.ShapeDtypeStruct((1, RANK, RANK), f32)
    return pl.pallas_call(
        kernel_body,
        out_shape=(jax.ShapeDtypeStruct((leaves, RANK, RANK), f32), panel, panel),
        in_specs=[SMEM] * 3 + [ANY] * 6,
        out_specs=(VMEM, VMEM, VMEM),
        scratch_shapes=[
            pltpu.VMEM((leaves, width, width), bf16),
            pltpu.VMEM((leaves, 1, width, width), bf16),
            pltpu.VMEM((leaves, width, width), bf16),
            pltpu.VMEM((leaves, entries, RANK, RANK), bf16),
            pltpu.VMEM((RING, RING, HALF, RANK), bf16),
            pltpu.VMEM((RING, RING, HALF, RANK), bf16),
            pltpu.VMEM((2 * leaves, width, RANK), bf16),
            pltpu.VMEM((RING, RANK, RANK), f32),
            pltpu.VMEM((leaves, width, width), f32),
            pltpu.VMEM((leaves, RANK, RANK), f32),
            pltpu.VMEM((leaves * entries, RANK, RANK), bf16),
            pltpu.VMEM((leaves * entries + 1, RANK, RANK), bf16),
            pltpu.VMEM((2, RING, RING, HALF, RANK), bf16),
            pltpu.VMEM((2, SIZE, RING, HALF, RANK), bf16),
            pltpu.VMEM((2, SIZE - 1, RING, HALF, RANK), bf16),
            pltpu.VMEM((2, RING, HALF, RANK), bf16),
            pltpu.VMEM((2, RING, HALF, RANK), bf16),
            pltpu.VMEM((RANK, RANK), f32),
            pltpu.VMEM((RING, RANK, RANK), bf16),
            pltpu.VMEM((2, RING * RANK, RANK), bf16),
            pltpu.VMEM((RANK, RANK), f32),
            pltpu.VMEM((2, DEPTH, RANK), f32),
            pltpu.VMEM((3, RING, DEPTH, RANK), f32),
            sems((2 * leaves + 5,)),
            sems((3, RING)), sems((3, RING)),
            sems((2, 2, SIZE + 1)), sems((2, 2, SIZE + 1)),
            sems((2, 2, SIZE + 1, PIECES)), sems((2, 2, SIZE + 1, PIECES)),
            sems((2, RING)), sems((2, RING)),
            sems((RING,)), sems((RING,)),
            sems((3, RING)), sems((3, RING)),
        ],
        compiler_params=pltpu.CompilerParams(
            collective_id=0, has_side_effects=True, vmem_limit_bytes=48 * 2**20
        ),
    )(near_list, adm_list, inverse, self_blocks, near_blocks, leaf_basis, transfer, parent_kernel, chain_coupling)


def solution(mesh):
    lead = P(("grp", "leaf"))
    return jax.shard_map(
        per_device,
        mesh=mesh,
        in_specs=(lead, lead, lead, lead, lead, lead, lead, P("grp")),
        out_specs=(lead, lead, P("grp")),
        check_vma=False,
    )
```

```python
import functools

import jax
import jax.numpy as jnp
from jax import lax
from jax.experimental import pallas as pl
from jax.experimental.pallas import tpu as pltpu
from jax.sharding import PartitionSpec as P

f32 = jnp.float32
bf16 = jnp.bfloat16
MESH = pl.DeviceIdType.MESH
VMEM = pl.BlockSpec(memory_space=pltpu.VMEM)
SMEM = pl.BlockSpec(memory_space=pltpu.SMEM)
ANY = pl.BlockSpec(memory_space=pl.ANY)
HBM = pl.BlockSpec(memory_space=pltpu.HBM)
RING = 8
RANK = 128
HALF = 64
TILE = (8, 128)


def dot(a, b):
    return jnp.dot(a, b, preferred_element_type=f32)


def dot_t(a, b):
    return lax.dot_general(a, b, (((0,), (0,)), ((), ())), preferred_element_type=f32)


def dot_full(a, b):
    return jnp.dot(a, b, precision=lax.Precision.HIGHEST, preferred_element_type=f32)


def dot_t_full(a, b):
    return lax.dot_general(
        a, b, (((0,), (0,)), ((), ())), precision=lax.Precision.HIGHEST, preferred_element_type=f32
    )


def split(x):
    high = x.astype(bf16)
    return high, (x - high.astype(f32)).astype(bf16)


def dot_split(a, b):
    (ah, al), (bh, bl) = split(a), split(b)
    return dot(ah, bh) + (dot(ah, bl) + dot(al, bh))


def invert(first, second, between):
    sub = lax.broadcasted_iota(jnp.int32, TILE, 0)
    lane = lax.broadcasted_iota(jnp.int32, TILE, 1)
    lane_all = lax.broadcasted_iota(jnp.int32, (RANK, RANK), 1)
    upper_half = sub < 4
    turn = lambda x: pltpu.roll(x, 4, axis=0)
    pack = lambda x, y: (jnp.where(upper_half, x, turn(y)), jnp.where(upper_half, turn(x), y))
    spread = lambda x, j: jnp.take_along_axis(x, jnp.where(upper_half, j, 4 + j), axis=0)
    steps = RANK // 8
    strip = pack(first[0:8], second[0:8])
    for s in range(steps):
        c0 = 8 * s
        last = s + 1 == steps
        inside = (lane >= c0) & (lane < c0 + 8)
        column = lambda x, i: jnp.broadcast_to(x[:, c0 + i : c0 + i + 1], TILE)
        columns = [[column(x, i) for i in range(8)] for x in strip]
        block = {(j, i): spread(columns[j // 4][i], j % 4) for i in range(8) for j in range(i, 8)}
        rows = [
            jnp.where(inside, jnp.where(lane == c0 + j, 1.0, 0.0), spread(strip[j // 4], j % 4)) for j in range(8)
        ]
        if not last:
            below = pack(first[c0 + 8 : c0 + 16], second[c0 + 8 : c0 + 16])
            left = [[column(x, i) for i in range(8)] for x in below]
            following = [jnp.where(inside, 0.0, x) for x in below]
        mult = {}
        for k in range(8):
            pivot = 1.0 / block[k, k]
            for j in range(k + 1, 8):
                mult[j, k] = block[j, k] * pivot
            for j in range(k + 1, 8):
                for i in range(k + 1, j + 1):
                    block[j, i] = block[j, i] - mult[j, k] * block[i, k]
                rows[j] = rows[j] - mult[j, k] * rows[k]
            rows[k] = rows[k] * pivot
            if not last:
                for q in range(2):
                    following[q] = following[q] - left[q][k] * rows[k]
                    for j in range(k + 1, 8):
                        left[q][j] = left[q][j] - mult[j, k] * left[q][k]
        for k in range(7, 0, -1):
            for j in range(k):
                rows[j] = rows[j] - mult[k, j] * rows[k]
        kept, turned = rows[0], rows[4]
        for j in range(1, 8):
            kept = jnp.where(sub == j, rows[j], kept)
            turned = jnp.where(sub == j, rows[(j + 4) % 8], turned)
        turned = turn(turned)
        inside_all = (lane_all >= c0) & (lane_all < c0 + 8)
        nothing = jnp.zeros(TILE, f32)
        results = []
        for a, done in (
            (first, jnp.where(upper_half, kept, turned)),
            (second, jnp.where(upper_half, turned, kept)),
        ):
            high = done.astype(bf16).astype(f32)
            place = lambda x: jnp.concatenate([x if t == s else nothing for t in range(steps)], axis=0).astype(bf16)
            zh, zl = place(high), place(done - high)
            wide = jnp.concatenate(
                [
                    jnp.concatenate([zh, zl], axis=1),
                    jnp.concatenate([zh, jnp.zeros((RANK, RANK), bf16)], axis=1),
                ],
                axis=0,
            )
            product = dot(jnp.concatenate(split(a), axis=1), wide)
            rest = jnp.where(inside_all, 0.0, a) - (product[:, :RANK] + product[:, RANK:])
            results.append(
                jnp.concatenate([done if t == s else rest[8 * t : 8 * t + 8] for t in range(steps)], axis=0)
            )
        first, second = results
        if not last:
            strip = following
        between(s)
    return first, second


def form_reduced(l, parts, blocks, basis, reduced):
    turned = dot(blocks[l], basis[l]).astype(bf16)
    reduced[l] = dot_t(turned, basis[l])
    for i in range(parts - 1):
        for j in range(i, parts - 1):
            si, sj = pl.ds(RANK * i, RANK), pl.ds(RANK * j, RANK)
            x = 0.5 * (reduced[l, si, sj] + reduced[l, sj, si].T)
            reduced[l, si, sj] = x
            if j > i:
                reduced[l, sj, si] = x.T


def eliminate(leaves, parts, reduced, inverses, between):
    @pl.loop(0, parts - 1)
    def _(k):
        here = pl.ds(pl.multiple_of(k * RANK, RANK), RANK)
        inverses[0], inverses[1] = invert(reduced[0, here, here], reduced[1, here, here], functools.partial(between, k))
        for known in range(parts - 1):

            @pl.when(k == known)
            def _(known=known):
                here = pl.ds(RANK * known, RANK)
                rest = pl.ds(RANK * (known + 1), RANK * (parts - 1 - known))
                for l in range(leaves):
                    solved = dot_split(inverses[l], reduced[l, here, rest])
                    reduced[l, rest, rest] = reduced[l, rest, rest] - dot_split(reduced[l, rest, here], solved)


class Places:
    def __init__(self):
        self.grp = lax.axis_index("grp")
        self.leaf = lax.axis_index("leaf")
        self.z = self.leaf // RING
        self.y = self.leaf % RING

    def on_z(self, z):
        return (self.grp, z * RING + self.y)

    def on_y(self, y):
        return (self.grp, self.z * RING + y)

    def on_grp(self, grp):
        return (grp, self.leaf)

    def on_leaf(self, step):
        n = lax.axis_size("leaf")
        return (self.grp, (self.leaf + step + n) % n)


def others(pos):
    return [(pos + o) % RING for o in range(1, RING)]


def partners(at):
    ids = [at.on_z(i) for i in others(at.z)] + [at.on_y(i) for i in others(at.y)]
    return ids + [at.on_grp(i) for i in others(at.grp)] + [at.on_leaf(1), at.on_leaf(-1)]


def greet(at):
    for i in partners(at):
        pl.semaphore_signal(pltpu.get_barrier_semaphore(), inc=1, device_id=i, device_id_type=MESH)


def await_greetings(at):
    pl.semaphore_wait(pltpu.get_barrier_semaphore(), len(partners(at)))


def remote(src, dst, send, recv, to):
    return pltpu.make_async_remote_copy(
        src_ref=src, dst_ref=dst, send_sem=send, recv_sem=recv, device_id=to, device_id_type=MESH
    )


def exchange(pos, to, src, dst, send, recv):
    copies = []
    for o in range(1, RING):
        i = (pos + o) % RING
        copy = remote(src(i), dst.at[pos], send.at[o], recv.at[o], to(i))
        copy.start()
        copies.append(copy)
    return copies


def wait_all(copies):
    for copy in copies:
        copy.wait()


SIZE = RING // 2
PIECES = 2
DEPTH = RANK // RING
SPAN = RING // PIECES
GATHER_AT = [
    ((0, 3), 1, 0), ((0, 3), 1, 1), ((1, 0), 2, 0), ((1, 2), 2, 1),
    ((1, 14), 3, 0), ((2, 0), 3, 1), ((2, 10), 4, 0), ((2, 13), 4, 1),
]


def kernel_body(
    table, blocks_hbm, near_hbm, basis_hbm, transfer_hbm, kernel_hbm, chain_hbm,
    panels_ref, parent_ref, top_ref,
    blocks, near, basis, transfer, upper, lower, halo, maps, reduced, inverses, lifted, terms, shares,
    down_in, up_in, near_sum, far_in, local, local_in, prefix, cross, slabs, slab_in,
    load_sem, send_1, recv_1, send_2, recv_2, send_c, recv_c, send_f, recv_f, send_g, recv_g, send_r, recv_r,
):
    at = Places()
    leaves, width = basis.shape[:2]
    entries = transfer.shape[1]
    parts = width // RANK
    skeleton = pl.ds(width - RANK, RANK)
    lines = ((at.z, at.on_z), (at.y, at.on_y))

    top = kernel_hbm.at[0, pl.ds(0, HALF)]
    bottom = kernel_hbm.at[0, pl.ds(HALF, HALF)]
    loads = []
    for l in range(leaves):
        loads += [(basis_hbm.at[l], basis.at[l]), (blocks_hbm.at[l], blocks.at[l])]
    loads += [(near_hbm, near), (transfer_hbm, transfer)]
    loads += [(top, upper.at[at.y, at.z]), (bottom, lower.at[at.z, at.y]), (chain_hbm.at[0], maps.at[at.grp])]
    loads = [pltpu.make_async_copy(src, dst, load_sem.at[i]) for i, (src, dst) in enumerate(loads)]
    greet(at)
    for load in loads:
        load.start()
    await_greetings(at)
    exchange(at.z, at.on_z, lambda i: top, upper.at[at.y], send_1.at[0], recv_1.at[0])
    exchange(at.y, at.on_y, lambda i: bottom, lower.at[at.z], send_1.at[1], recv_1.at[1])
    exchange(at.grp, at.on_grp, lambda i: chain_hbm.at[0], maps, send_1.at[2], recv_1.at[2])

    for l in range(leaves):
        loads[2 * l].wait()
        loads[2 * l + 1].wait()
        form_reduced(l, parts, blocks, basis, reduced)

    def gather_copies(t, u):
        copies = []
        piece = pl.ds(u * SPAN, SPAN)
        for h, (table, pos, to) in enumerate(((upper, at.y, at.on_y), (lower, at.z, at.on_z))):
            for up in range(2):
                if t == SIZE and not up:
                    continue
                chunk = (pos - t + 1 + RING) % RING if up else (pos + t - 1) % RING
                target = (pos + 1) % RING if up else (pos + RING - 1) % RING
                part = table.at[chunk, piece]
                copies.append(remote(part, part, send_2.at[h, up, t, u], recv_2.at[h, up, t, u], to(target)))
        return copies

    def halo_copies():
        source = basis.at[:, :, skeleton]
        return [
            remote(source, halo.at[pl.ds(0, leaves)], send_1.at[0, 0], recv_1.at[0, 0], at.on_leaf(1)),
            remote(source, halo.at[pl.ds(leaves, leaves)], send_1.at[1, 0], recv_1.at[1, 0], at.on_leaf(-1)),
        ]

    def first_copies():
        return [
            remote(top, upper.at[at.y, at.z], send_1.at[0, o], recv_1.at[0, o], at.on_z((at.z + o) % RING))
            for o in range(1, RING)
        ] + [
            remote(bottom, lower.at[at.z, at.y], send_1.at[1, o], recv_1.at[1, o], at.on_y((at.y + o) % RING))
            for o in range(1, RING)
        ]

    def between(k, s):
        for (block, step), t, u in GATHER_AT:
            if s == step:

                @pl.when(k == block)
                def _(t=t, u=u):
                    if t > 1:
                        for copy in gather_copies(t - 1, u):
                            copy.wait_recv()
                    elif u == 0:
                        loads[-3].wait()
                        loads[-2].wait()
                        wait_all(first_copies())
                    for copy in gather_copies(t, u):
                        copy.start()
                    if t == SIZE and u == PIECES - 1:
                        for copy in halo_copies():
                            copy.start()

    eliminate(leaves, parts, reduced, inverses, between)

    loads[2 * leaves + 1].wait()
    group = 8
    for l in range(leaves):
        lowered = reduced[l, skeleton, skeleton].astype(bf16)

        @pl.loop(0, entries // group)
        def _(step, l=l, lowered=lowered):
            for i in range(group):
                a = step * group + i
                lifted[l * entries + a] = dot(lowered, transfer[l, a]).astype(bf16)

    for u in range(PIECES):
        for copy in gather_copies(SIZE, u):
            copy.wait_recv()
    local[...] = jnp.zeros_like(local)

    for l in range(leaves):

        @pl.loop(0, entries // group)
        def _(step, l=l):
            total = None
            for i in range(group):
                a = step * group + i
                p = table[l, RING * RING + a]
                pz, py = p // RING, p % RING
                panel = lifted[l * entries + a]
                kernel = jnp.concatenate([upper[py, pz], lower[pz, py]], axis=0)
                mixture = dot(kernel, panel).astype(bf16)
                term = dot_t(panel, mixture)
                terms[l * entries + a] = term.astype(bf16)
                total = term if total is None else total + term
            local[...] += total

    terms[leaves * entries] = jnp.zeros((RANK, RANK), bf16)
    local_in[at.grp] = local[...].astype(bf16)
    by_grp = exchange(at.grp, at.on_grp, lambda i: local_in.at[at.grp], local_in, send_g, recv_g)

    @pl.loop(0, RING)
    def _(pz):
        for py in range(RING):
            p = pz * RING + py
            share = terms[table[0, p]].astype(f32)
            for l in range(1, leaves):
                share = share + terms[table[l, p]].astype(f32)
            share = share.astype(bf16)
            shares[0, pz, py] = share[:HALF]
            shares[1, py, pz] = share[HALF:]

    def chain_copy(h, up, t, u):
        pos, to = lines[h]
        piece = pl.ds(u * SPAN, SPAN)
        buffer = (down_in, up_in)[up]
        chunk = (pos + 4 - t + RING) % RING if up else (pos - 5 + t + RING) % RING
        src = shares.at[h, chunk, piece] if t == 1 else buffer.at[h, t - 2, piece]
        target = (pos + 1) % RING if up else (pos + RING - 1) % RING
        return remote(src, buffer.at[h, t - 1, piece], send_c.at[h, up, t, u], recv_c.at[h, up, t, u], to(target))

    def chain_step(t):
        for u in range(PIECES):
            for h in range(2):
                pos, _ = lines[h]
                for up in range(2):
                    if t > 1:
                        chain_copy(h, up, t - 1, u).wait_recv()
                    if up and t == SIZE:
                        continue
                    if t > 1:
                        piece = pl.ds(u * SPAN, SPAN)
                        buffer = (down_in, up_in)[up]
                        chunk = (pos + 4 - t + RING) % RING if up else (pos - 5 + t + RING) % RING
                        mine = shares[h, chunk, piece].astype(f32)
                        buffer[h, t - 2, piece] = (buffer[h, t - 2, piece].astype(f32) + mine).astype(bf16)
                    chain_copy(h, up, t, u).start()

    chain_step(1)

    wait_all(
        [
            remote(chain_hbm.at[0], maps.at[at.grp], send_1.at[2, o], recv_1.at[2, o], at.on_grp((at.grp + o) % RING))
            for o in range(1, RING)
        ]
    )
    loads[-1].wait()
    eye = (
        lax.broadcasted_iota(jnp.int32, (RANK, RANK), 0) == lax.broadcasted_iota(jnp.int32, (RANK, RANK), 1)
    ).astype(f32)
    running = jnp.zeros((RANK, RANK), f32)
    for j in range(RING - 1, -1, -1):
        if j < RING - 1:
            step_map = 0.8 * eye + 0.5 * maps[j + 1]
            running = jnp.where(j < at.grp, dot_full(step_map, running), 0.0)
        running = jnp.where(j == at.grp, eye, running)
        high = running.astype(bf16)
        prefix[0, pl.ds(j * RANK, RANK)] = high
        prefix[1, pl.ds(j * RANK, RANK)] = (running - high.astype(f32)).astype(bf16)

    chain_step(2)

    wait_all(by_grp)
    mapped = jnp.concatenate(
        [
            dot(local_in[j], prefix[0, pl.ds(j * RANK, RANK)]) + dot(local_in[j], prefix[1, pl.ds(j * RANK, RANK)])
            for j in range(RING)
        ],
        axis=0,
    )
    high = mapped.astype(bf16)
    low = (mapped - high.astype(f32)).astype(bf16)
    cross[...] = (dot_t(prefix[0], high) + (dot_t(prefix[1], high) + dot_t(prefix[0], low))) * (1.0 / (RING * RING))

    slab = lambda i: pl.ds(pl.multiple_of(i * DEPTH, DEPTH), DEPTH)

    def gathered(stage, pos, mine):
        total = mine
        for o in range(1, RING):
            total = total + slab_in[stage, (pos + o) % RING]
        return total

    by_z = exchange(at.z, at.on_z, lambda i: cross.at[slab(i)], slab_in.at[0], send_r.at[0], recv_r.at[0])

    chain_step(3)

    for copy in halo_copies():
        copy.wait()
    loads[2 * leaves].wait()
    first = ((at.grp * lax.axis_size("leaf") + at.leaf) - 1) * leaves
    for l in range(leaves):
        place = table[l, RING * RING + entries] - first
        place = jnp.clip(jnp.where(place < leaves, place, place - leaves), 0, 2 * leaves - 1)
        facing = dot_t(basis[l, :, skeleton], near[l, 0]).astype(bf16)
        panels_ref[l] = reduced[l, skeleton, skeleton] + dot(facing, halo[place])

    chain_step(4)
    wait_all(by_z)
    slabs[0] = gathered(0, at.z, cross[slab(at.z)])
    by_y = exchange(at.y, at.on_y, lambda i: slabs.at[0], slab_in.at[1], send_r.at[1], recv_r.at[1])

    def far_copy(h, i):
        other, to = lines[1 - h]
        return remote(near_sum.at[h, i], far_in.at[h, other], send_f.at[h, i], recv_f.at[h, other], to(i))

    for u in range(PIECES):
        piece = pl.ds(u * SPAN, SPAN)
        for h in range(2):
            pos, _ = lines[h]
            chain_copy(h, 0, SIZE, u).wait_recv()
            near_sum[h, piece] = (
                down_in[h, SIZE - 1, piece].astype(f32)
                + up_in[h, SIZE - 2, piece].astype(f32)
                + shares[h, pos, piece].astype(f32)
            ).astype(bf16)
            for i in range(u * SPAN, (u + 1) * SPAN):

                @pl.when(i != lines[1 - h][0])
                def _(h=h, i=i):
                    far_copy(h, i).start()

    wait_all(by_y)
    slabs[1] = gathered(1, at.y, slabs[0])
    again = exchange(at.z, at.on_z, lambda i: slabs.at[1], slab_in.at[2], send_r.at[2], recv_r.at[2])
    for t in range(1, SIZE + 1):
        for u in range(PIECES):
            for copy in gather_copies(t, u):
                copy.wait_send()
    wait_all(again)
    slab_in[2, at.z] = slabs[1]
    for i in range(RING):
        top_ref[0, pl.ds(i * DEPTH, DEPTH)] = slab_in[2, i]
    for h in range(2):
        for up in range(2):
            for t in range(1, SIZE + 1 - up):
                for u in range(PIECES):
                    chain_copy(h, up, t, u).wait_send()
    for h in range(2):
        other, to = lines[1 - h]
        total = near_sum[h, other].astype(f32)
        for o in range(1, RING):
            i = (other + o) % RING
            far_copy(h, i).wait_send()
            remote(near_sum.at[h, i], far_in.at[h, i], send_f.at[h, i], recv_f.at[h, i], to(i)).wait_recv()
            total = total + far_in[h, i].astype(f32)
        parent_ref[0, pl.ds(h * HALF, HALF)] = total


def hand_out(*refs):
    for i in range(3):
        refs[3 + i][...] = refs[i][...]


def per_device(self_blocks, near_blocks, leaf_basis, transfer, near_list, adm_list, parent_kernel, chain_coupling):
    leaves, width = leaf_basis.shape[:2]
    entries = transfer.shape[1]
    order = jnp.arange(leaves * entries, dtype=jnp.int32).reshape(leaves, entries, 1)
    names = adm_list[:, :, None] == jnp.arange(RING * RING, dtype=jnp.int32)[None, None, :]
    inverse = jnp.min(jnp.where(names, order, leaves * entries), axis=1)
    table = jnp.concatenate([inverse, adm_list, near_list], axis=1)
    sems = pltpu.SemaphoreType.DMA
    panel = jax.ShapeDtypeStruct((1, RANK, RANK), f32)
    results = pl.pallas_call(
        kernel_body,
        out_shape=(jax.ShapeDtypeStruct((leaves, RANK, RANK), f32), panel, panel),
        in_specs=[SMEM] + [HBM] * 6,
        out_specs=(VMEM, VMEM, VMEM),
        scratch_shapes=[
            pltpu.VMEM((leaves, width, width), bf16),
            pltpu.VMEM((leaves, 1, width, width), bf16),
            pltpu.VMEM((leaves, width, width), bf16),
            pltpu.VMEM((leaves, entries, RANK, RANK), bf16),
            pltpu.VMEM((RING, RING, HALF, RANK), bf16),
            pltpu.VMEM((RING, RING, HALF, RANK), bf16),
            pltpu.VMEM((2 * leaves, width, RANK), bf16),
            pltpu.VMEM((RING, RANK, RANK), f32),
            pltpu.VMEM((leaves, width, width), f32),
            pltpu.VMEM((leaves, RANK, RANK), f32),
            pltpu.VMEM((leaves * entries, RANK, RANK), bf16),
            pltpu.VMEM((leaves * entries + 1, RANK, RANK), bf16),
            pltpu.VMEM((2, RING, RING, HALF, RANK), bf16),
            pltpu.VMEM((2, SIZE, RING, HALF, RANK), bf16),
            pltpu.VMEM((2, SIZE - 1, RING, HALF, RANK), bf16),
            pltpu.VMEM((2, RING, HALF, RANK), bf16),
            pltpu.VMEM((2, RING, HALF, RANK), bf16),
            pltpu.VMEM((RANK, RANK), f32),
            pltpu.VMEM((RING, RANK, RANK), bf16),
            pltpu.VMEM((2, RING * RANK, RANK), bf16),
            pltpu.VMEM((RANK, RANK), f32),
            pltpu.VMEM((2, DEPTH, RANK), f32),
            pltpu.VMEM((3, RING, DEPTH, RANK), f32),
            sems((2 * leaves + 5,)),
            sems((3, RING)), sems((3, RING)),
            sems((2, 2, SIZE + 1, PIECES)), sems((2, 2, SIZE + 1, PIECES)),
            sems((2, 2, SIZE + 1, PIECES)), sems((2, 2, SIZE + 1, PIECES)),
            sems((2, RING)), sems((2, RING)),
            sems((RING,)), sems((RING,)),
            sems((3, RING)), sems((3, RING)),
        ],
        compiler_params=pltpu.CompilerParams(
            collective_id=0, has_side_effects=True, vmem_limit_bytes=58 * 2**20
        ),
    )(table, self_blocks, near_blocks, leaf_basis, transfer, parent_kernel, chain_coupling)
    return pl.pallas_call(
        hand_out,
        out_shape=tuple(jax.ShapeDtypeStruct(r.shape, r.dtype) for r in results),
        in_specs=[VMEM] * 3,
        out_specs=(VMEM,) * 3,
        compiler_params=pltpu.CompilerParams(vmem_limit_bytes=58 * 2**20),
    )(*results)


def solution(mesh):
    lead = P(("grp", "leaf"))
    return jax.shard_map(
        per_device,
        mesh=mesh,
        in_specs=(lead, lead, lead, lead, lead, lead, lead, P("grp")),
        out_specs=(lead, lead, P("grp")),
        check_vma=False,
    )
```

```python
import functools

import jax
import jax.numpy as jnp
from jax import lax
from jax.experimental import pallas as pl
from jax.experimental.pallas import tpu as pltpu
from jax.sharding import PartitionSpec as P

f32 = jnp.float32
bf16 = jnp.bfloat16
MESH = pl.DeviceIdType.MESH
VMEM = pl.BlockSpec(memory_space=pltpu.VMEM)
SMEM = pl.BlockSpec(memory_space=pltpu.SMEM)
ANY = pl.BlockSpec(memory_space=pl.ANY)
HBM = pl.BlockSpec(memory_space=pltpu.HBM)
RING = 8
RANK = 128
HALF = 64
TILE = (8, 128)


def dot(a, b):
    return jnp.dot(a, b, preferred_element_type=f32)


def dot_t(a, b):
    return lax.dot_general(a, b, (((0,), (0,)), ((), ())), preferred_element_type=f32)


def dot_full(a, b):
    return jnp.dot(a, b, precision=lax.Precision.HIGHEST, preferred_element_type=f32)


def dot_t_full(a, b):
    return lax.dot_general(
        a, b, (((0,), (0,)), ((), ())), precision=lax.Precision.HIGHEST, preferred_element_type=f32
    )


def split(x):
    high = x.astype(bf16)
    return high, (x - high.astype(f32)).astype(bf16)


def dot_split(a, b):
    (ah, al), (bh, bl) = split(a), split(b)
    return dot(ah, bh) + (dot(ah, bl) + dot(al, bh))


def invert(first, second, between):
    sub = lax.broadcasted_iota(jnp.int32, TILE, 0)
    lane = lax.broadcasted_iota(jnp.int32, TILE, 1)
    lane_all = lax.broadcasted_iota(jnp.int32, (RANK, RANK), 1)
    upper_half = sub < 4
    turn = lambda x: pltpu.roll(x, 4, axis=0)
    pack = lambda x, y: (jnp.where(upper_half, x, turn(y)), jnp.where(upper_half, turn(x), y))
    spread = lambda x, j: jnp.take_along_axis(x, jnp.where(upper_half, j, 4 + j), axis=0)
    steps = RANK // 8
    strip = pack(first[0:8], second[0:8])
    for s in range(steps):
        c0 = 8 * s
        last = s + 1 == steps
        inside = (lane >= c0) & (lane < c0 + 8)
        column = lambda x, i: jnp.broadcast_to(x[:, c0 + i : c0 + i + 1], TILE)
        columns = [[column(x, i) for i in range(8)] for x in strip]
        block = {(j, i): spread(columns[j // 4][i], j % 4) for i in range(8) for j in range(i, 8)}
        rows = [
            jnp.where(inside, jnp.where(lane == c0 + j, 1.0, 0.0), spread(strip[j // 4], j % 4)) for j in range(8)
        ]
        if not last:
            below = pack(first[c0 + 8 : c0 + 16], second[c0 + 8 : c0 + 16])
            left = [[column(x, i) for i in range(8)] for x in below]
            following = [jnp.where(inside, 0.0, x) for x in below]
        mult = {}
        for k in range(8):
            pivot = 1.0 / block[k, k]
            for j in range(k + 1, 8):
                mult[j, k] = block[j, k] * pivot
            for j in range(k + 1, 8):
                for i in range(k + 1, j + 1):
                    block[j, i] = block[j, i] - mult[j, k] * block[i, k]
                rows[j] = rows[j] - mult[j, k] * rows[k]
            rows[k] = rows[k] * pivot
            if not last:
                for q in range(2):
                    following[q] = following[q] - left[q][k] * rows[k]
                    for j in range(k + 1, 8):
                        left[q][j] = left[q][j] - mult[j, k] * left[q][k]
        for k in range(7, 0, -1):
            for j in range(k):
                rows[j] = rows[j] - mult[k, j] * rows[k]
        kept, turned = rows[0], rows[4]
        for j in range(1, 8):
            kept = jnp.where(sub == j, rows[j], kept)
            turned = jnp.where(sub == j, rows[(j + 4) % 8], turned)
        turned = turn(turned)
        inside_all = (lane_all >= c0) & (lane_all < c0 + 8)
        nothing = jnp.zeros(TILE, f32)
        results = []
        for a, done in (
            (first, jnp.where(upper_half, kept, turned)),
            (second, jnp.where(upper_half, turned, kept)),
        ):
            high = done.astype(bf16).astype(f32)
            place = lambda x: jnp.concatenate([x if t == s else nothing for t in range(steps)], axis=0).astype(bf16)
            zh, zl = place(high), place(done - high)
            wide = jnp.concatenate(
                [
                    jnp.concatenate([zh, zl], axis=1),
                    jnp.concatenate([zh, jnp.zeros((RANK, RANK), bf16)], axis=1),
                ],
                axis=0,
            )
            product = dot(jnp.concatenate(split(a), axis=1), wide)
            rest = jnp.where(inside_all, 0.0, a) - (product[:, :RANK] + product[:, RANK:])
            results.append(
                jnp.concatenate([done if t == s else rest[8 * t : 8 * t + 8] for t in range(steps)], axis=0)
            )
        first, second = results
        if not last:
            strip = following
        between(s)
    return first, second


def form_reduced(l, parts, blocks, basis, reduced):
    turned = dot(blocks[l], basis[l]).astype(bf16)
    reduced[l] = dot_t(turned, basis[l])
    for i in range(parts - 1):
        for j in range(i, parts - 1):
            si, sj = pl.ds(RANK * i, RANK), pl.ds(RANK * j, RANK)
            x = 0.5 * (reduced[l, si, sj] + reduced[l, sj, si].T)
            reduced[l, si, sj] = x
            if j > i:
                reduced[l, sj, si] = x.T


def eliminate(leaves, parts, reduced, inverses, between):
    @pl.loop(0, parts - 1)
    def _(k):
        here = pl.ds(pl.multiple_of(k * RANK, RANK), RANK)
        inverses[0], inverses[1] = invert(reduced[0, here, here], reduced[1, here, here], functools.partial(between, k))
        for known in range(parts - 1):

            @pl.when(k == known)
            def _(known=known):
                here = pl.ds(RANK * known, RANK)
                rest = pl.ds(RANK * (known + 1), RANK * (parts - 1 - known))
                for l in range(leaves):
                    solved = dot_split(inverses[l], reduced[l, here, rest])
                    reduced[l, rest, rest] = reduced[l, rest, rest] - dot_split(reduced[l, rest, here], solved)


class Places:
    def __init__(self):
        self.grp = lax.axis_index("grp")
        self.leaf = lax.axis_index("leaf")
        self.z = self.leaf // RING
        self.y = self.leaf % RING

    def on_z(self, z):
        return (self.grp, z * RING + self.y)

    def on_y(self, y):
        return (self.grp, self.z * RING + y)

    def on_grp(self, grp):
        return (grp, self.leaf)

    def on_leaf(self, step):
        n = lax.axis_size("leaf")
        return (self.grp, (self.leaf + step + n) % n)


def others(pos):
    return [(pos + o) % RING for o in range(1, RING)]


def partners(at):
    ids = [at.on_z(i) for i in others(at.z)] + [at.on_y(i) for i in others(at.y)]
    return ids + [at.on_grp(i) for i in others(at.grp)] + [at.on_leaf(1), at.on_leaf(-1)]


def greet(at):
    for i in partners(at):
        pl.semaphore_signal(pltpu.get_barrier_semaphore(), inc=1, device_id=i, device_id_type=MESH)


def await_greetings(at):
    pl.semaphore_wait(pltpu.get_barrier_semaphore(), len(partners(at)))


def remote(src, dst, send, recv, to):
    return pltpu.make_async_remote_copy(
        src_ref=src, dst_ref=dst, send_sem=send, recv_sem=recv, device_id=to, device_id_type=MESH
    )


def exchange(pos, to, src, dst, send, recv):
    copies = []
    for o in range(1, RING):
        i = (pos + o) % RING
        copy = remote(src(i), dst.at[pos], send.at[o], recv.at[o], to(i))
        copy.start()
        copies.append(copy)
    return copies


def wait_all(copies):
    for copy in copies:
        copy.wait()


SIZE = RING // 2
PIECES = 2
DEPTH = RANK // RING
SPAN = RING // PIECES
GATHER_AT = [
    ((0, 14), 2, 0), ((0, 15), 2, 1), ((1, 11), 3, 0), ((1, 13), 3, 1), ((2, 11), 4, 0), ((2, 13), 4, 1),
]


def kernel_body(
    adm, near_list, blocks_hbm, near_hbm, basis_hbm, transfer_hbm, kernel_hbm, chain_hbm,
    panels_hbm, parent_hbm, top_hbm,
    blocks, near, basis, transfer, upper, lower, halo, maps, reduced, inverses, lifted, terms, shares,
    down_in, up_in, near_sum, far_in, facing, local_in, prefix, prefix_t, cross, slabs, slab_in, inverse, where, panels_ref, parent_ref, top_ref,
    load_sem, send_1, recv_1, send_2, recv_2, send_c, recv_c, send_f, recv_f, send_g, recv_g, send_r, recv_r, out_sem,
):
    at = Places()
    leaves, width = basis.shape[:2]
    entries = transfer.shape[1]
    parts = width // RANK
    skeleton = pl.ds(width - RANK, RANK)
    lines = ((at.z, at.on_z), (at.y, at.on_y))

    top = kernel_hbm.at[0, pl.ds(0, HALF)]
    bottom = kernel_hbm.at[0, pl.ds(HALF, HALF)]
    loads = []
    for l in range(leaves):
        loads += [(basis_hbm.at[l], basis.at[l]), (blocks_hbm.at[l], blocks.at[l])]
    loads += [(near_hbm, near), (transfer_hbm, transfer)]
    loads += [(top, upper.at[at.y, at.z]), (bottom, lower.at[at.z, at.y]), (chain_hbm.at[0], maps.at[at.grp])]
    loads = [pltpu.make_async_copy(src, dst, load_sem.at[i]) for i, (src, dst) in enumerate(loads)]
    results = ((panels_ref, panels_hbm), (parent_ref, parent_hbm), (top_ref, top_hbm))
    results = [pltpu.make_async_copy(src, dst, out_sem.at[i]) for i, (src, dst) in enumerate(results)]
    greet(at)
    loads[0].start()
    loads[1].start()
    await_greetings(at)
    exchange(at.z, at.on_z, lambda i: top, upper.at[at.y], send_1.at[0], recv_1.at[0])
    exchange(at.y, at.on_y, lambda i: bottom, lower.at[at.z], send_1.at[1], recv_1.at[1])
    for load in loads[2 : 2 * leaves] + loads[-3:-1]:
        load.start()

    column = lax.broadcasted_iota(jnp.int32, TILE, 1)
    row = lax.broadcasted_iota(jnp.int32, TILE, 0)
    places = jnp.full(TILE, leaves * entries, jnp.int32)
    for l in range(leaves):
        for a in range(entries):
            places = jnp.where((column == adm[l, a]) & (row == l), l * entries + a, places)
    inverse[...] = places
    to_scalars = pltpu.make_async_copy(inverse, where, load_sem.at[2 * leaves + 5])
    to_scalars.start()

    for l in range(leaves):
        loads[2 * l].wait()
        loads[2 * l + 1].wait()
        form_reduced(l, parts, blocks, basis, reduced)

    def gather_copies(t, u):
        copies = []
        piece = pl.ds(u * SPAN, SPAN)
        for h, (table, pos, to) in enumerate(((upper, at.y, at.on_y), (lower, at.z, at.on_z))):
            for up in range(2):
                if t == SIZE and not up:
                    continue
                chunk = (pos - t + 1 + RING) % RING if up else (pos + t - 1) % RING
                target = (pos + 1) % RING if up else (pos + RING - 1) % RING
                part = table.at[chunk, piece]
                copies.append(remote(part, part, send_2.at[h, up, t, u], recv_2.at[h, up, t, u], to(target)))
        return copies

    def halo_copies():
        source = basis.at[:, :, skeleton]
        return [
            remote(source, halo.at[pl.ds(0, leaves)], send_1.at[0, 0], recv_1.at[0, 0], at.on_leaf(1)),
            remote(source, halo.at[pl.ds(leaves, leaves)], send_1.at[1, 0], recv_1.at[1, 0], at.on_leaf(-1)),
        ]

    def first_copies():
        return [
            remote(top, upper.at[at.y, at.z], send_1.at[0, o], recv_1.at[0, o], at.on_z((at.z + o) % RING))
            for o in range(1, RING)
        ] + [
            remote(bottom, lower.at[at.z, at.y], send_1.at[1, o], recv_1.at[1, o], at.on_y((at.y + o) % RING))
            for o in range(1, RING)
        ]

    def between(k, s):
        for (block, step), t, u in GATHER_AT:
            if s == step:

                @pl.when(k == block)
                def _(t=t, u=u):
                    for copy in gather_copies(t - 1, u):
                        copy.wait_recv()
                    for copy in gather_copies(t, u):
                        copy.start()
                    if (t, u) == (2, PIECES - 1):
                        exchange(at.grp, at.on_grp, lambda i: chain_hbm.at[0], maps, send_1.at[2], recv_1.at[2])

        if s == 4:

            @pl.when(k == 1)
            def _():
                loads[2 * leaves].wait()
                for l in range(leaves):
                    facing[l] = dot_t(basis[l, :, skeleton], near[l, 0]).astype(bf16)

    loads[-3].wait()
    loads[-2].wait()
    wait_all(first_copies())
    for u in range(PIECES):
        for copy in gather_copies(1, u):
            copy.start()
    for load in (loads[2 * leaves], loads[2 * leaves + 1], loads[-1]):
        load.start()
    eliminate(leaves, parts, reduced, inverses, between)

    loads[2 * leaves + 1].wait()
    for l in range(leaves):
        lowered = reduced[l, skeleton, skeleton].astype(bf16)
        for a in range(0, entries, 2):
            pair = dot(lowered, jnp.concatenate([transfer[l, a], transfer[l, a + 1]], axis=1)).astype(bf16)
            lifted[l * entries + a] = pair[:, :RANK]
            lifted[l * entries + a + 1] = pair[:, RANK:]

    wait_all(
        [
            remote(chain_hbm.at[0], maps.at[at.grp], send_1.at[2, o], recv_1.at[2, o], at.on_grp((at.grp + o) % RING))
            for o in range(1, RING)
        ]
    )
    loads[-1].wait()
    eye = (
        lax.broadcasted_iota(jnp.int32, (RANK, RANK), 0) == lax.broadcasted_iota(jnp.int32, (RANK, RANK), 1)
    ).astype(f32)
    running = jnp.zeros((RANK, RANK), f32)
    for j in range(RING - 1, -1, -1):
        if j < RING - 1:
            step_map = 0.8 * eye + 0.5 * maps[j + 1]
            running = jnp.where(j < at.grp, dot_split(step_map, running), 0.0)
        running = jnp.where(j == at.grp, eye, running)
        prefix[j] = jnp.concatenate(split(running), axis=0)
        turned = split(running.T)
        for q in range(2):
            prefix_t[q, :, pl.ds(j * RANK, RANK)] = turned[q]

    for u in range(PIECES):
        for copy in gather_copies(SIZE, u):
            copy.wait_recv()
    for copy in halo_copies():
        copy.start()
    nothing = jnp.zeros((RANK, RANK), bf16)

    def diagonal(x, y):
        return jnp.concatenate(
            [jnp.concatenate([x, nothing], axis=1), jnp.concatenate([nothing, y], axis=1)], axis=0
        )

    total = None
    for l in range(leaves):
        for a in range(0, entries, 2):
            panels = [lifted[l * entries + a + q] for q in range(2)]
            kernels = []
            for q in range(2):
                p = adm[l, a + q]
                pz, py = p // RING, p % RING
                kernels.append(jnp.concatenate([upper[py, pz], lower[pz, py]], axis=0))
            mixture = dot(jnp.concatenate(kernels, axis=1), diagonal(*panels)).astype(bf16)
            term = dot(
                jnp.concatenate([panel.T for panel in panels], axis=1),
                diagonal(mixture[:, :RANK], mixture[:, RANK:]),
            )
            for q in range(2):
                part = term[:, q * RANK : (q + 1) * RANK]
                terms[l * entries + a + q] = part.astype(bf16)
                total = part if total is None else total + part

    terms[leaves * entries] = jnp.zeros((RANK, RANK), bf16)
    to_scalars.wait()
    local_in[at.grp] = total.astype(bf16)
    by_grp = exchange(at.grp, at.on_grp, lambda i: local_in.at[at.grp], local_in, send_g, recv_g)

    @pl.loop(0, RING)
    def _(pz):
        for py in range(RING):
            p = pz * RING + py
            share = terms[where[0, p]].astype(f32)
            for l in range(1, leaves):
                share = share + terms[where[l, p]].astype(f32)
            share = share.astype(bf16)
            shares[0, pz, py] = share[:HALF]
            shares[1, py, pz] = share[HALF:]

    def chain_copy(h, up, t, u):
        pos, to = lines[h]
        piece = pl.ds(u * SPAN, SPAN)
        buffer = (down_in, up_in)[up]
        chunk = (pos + 4 - t + RING) % RING if up else (pos - 5 + t + RING) % RING
        src = shares.at[h, chunk, piece] if t == 1 else buffer.at[h, t - 2, piece]
        target = (pos + 1) % RING if up else (pos + RING - 1) % RING
        return remote(src, buffer.at[h, t - 1, piece], send_c.at[h, up, t, u], recv_c.at[h, up, t, u], to(target))

    def chain_step(t):
        for u in range(PIECES):
            for h in range(2):
                pos, _ = lines[h]
                for up in range(2):
                    if t > 1:
                        chain_copy(h, up, t - 1, u).wait_recv()
                    if up and t == SIZE:
                        continue
                    if t > 1:
                        piece = pl.ds(u * SPAN, SPAN)
                        buffer = (down_in, up_in)[up]
                        chunk = (pos + 4 - t + RING) % RING if up else (pos - 5 + t + RING) % RING
                        mine = shares[h, chunk, piece].astype(f32)
                        buffer[h, t - 2, piece] = (buffer[h, t - 2, piece].astype(f32) + mine).astype(bf16)
                    chain_copy(h, up, t, u).start()

    chain_step(1)

    chain_step(2)

    wait_all(by_grp)
    mapped = []
    for j in range(RING):
        root = local_in[j]
        mapped.append(dot(jnp.concatenate([root, root], axis=1), prefix[j]))
    high, low = split(jnp.concatenate(mapped, axis=0))
    cross[...] = (dot(prefix_t[0], high) + (dot(prefix_t[1], high) + dot(prefix_t[0], low))) * (1.0 / (RING * RING))

    slab = lambda i: pl.ds(pl.multiple_of(i * DEPTH, DEPTH), DEPTH)

    def gathered(stage, pos, mine):
        total = mine
        for o in range(1, RING):
            total = total + slab_in[stage, (pos + o) % RING]
        return total

    by_z = exchange(at.z, at.on_z, lambda i: cross.at[slab(i)], slab_in.at[0], send_r.at[0], recv_r.at[0])

    chain_step(3)

    for copy in halo_copies():
        copy.wait()
    first = ((at.grp * lax.axis_size("leaf") + at.leaf) - 1) * leaves
    for l in range(leaves):
        place = near_list[0, l] - first
        place = jnp.clip(jnp.where(place < leaves, place, place - leaves), 0, 2 * leaves - 1)
        panels_ref[l] = reduced[l, skeleton, skeleton] + dot(facing[l], halo[place])
    results[0].start()

    wait_all(by_z)
    slabs[0] = gathered(0, at.z, cross[slab(at.z)])
    by_y = exchange(at.y, at.on_y, lambda i: slabs.at[0], slab_in.at[1], send_r.at[1], recv_r.at[1])
    chain_step(4)

    def far_copy(h, i):
        other, to = lines[1 - h]
        return remote(near_sum.at[h, i], far_in.at[h, other], send_f.at[h, i], recv_f.at[h, other], to(i))

    for u in range(PIECES):
        piece = pl.ds(u * SPAN, SPAN)
        for h in range(2):
            pos, _ = lines[h]
            chain_copy(h, 0, SIZE, u).wait_recv()
            near_sum[h, piece] = (
                down_in[h, SIZE - 1, piece].astype(f32)
                + up_in[h, SIZE - 2, piece].astype(f32)
                + shares[h, pos, piece].astype(f32)
            ).astype(bf16)
            for i in range(u * SPAN, (u + 1) * SPAN):

                @pl.when(i != lines[1 - h][0])
                def _(h=h, i=i):
                    far_copy(h, i).start()

    wait_all(by_y)
    slabs[1] = gathered(1, at.y, slabs[0])
    again = exchange(at.z, at.on_z, lambda i: slabs.at[1], slab_in.at[2], send_r.at[2], recv_r.at[2])
    for t in range(1, SIZE + 1):
        for u in range(PIECES):
            for copy in gather_copies(t, u):
                copy.wait_send()
    wait_all(again)
    slab_in[2, at.z] = slabs[1]
    for i in range(RING):
        top_ref[0, pl.ds(i * DEPTH, DEPTH)] = slab_in[2, i]
    results[2].start()
    for h in range(2):
        for up in range(2):
            for t in range(1, SIZE + 1 - up):
                for u in range(PIECES):
                    chain_copy(h, up, t, u).wait_send()
    for h in range(2):
        other, to = lines[1 - h]
        total = near_sum[h, other].astype(f32)
        for o in range(1, RING):
            i = (other + o) % RING
            far_copy(h, i).wait_send()
            remote(near_sum.at[h, i], far_in.at[h, i], send_f.at[h, i], recv_f.at[h, i], to(i)).wait_recv()
            total = total + far_in[h, i].astype(f32)
        parent_ref[0, pl.ds(h * HALF, HALF)] = total
    results[1].start()
    wait_all(results)


def hand_out(*refs):
    for i in range(3):
        refs[3 + i][...] = refs[i][...]


def per_device(self_blocks, near_blocks, leaf_basis, transfer, near_list, adm_list, parent_kernel, chain_coupling):
    leaves, width = leaf_basis.shape[:2]
    entries = transfer.shape[1]
    sems = pltpu.SemaphoreType.DMA
    panel = jax.ShapeDtypeStruct((1, RANK, RANK), f32)
    results = pl.pallas_call(
        kernel_body,
        out_shape=(jax.ShapeDtypeStruct((leaves, RANK, RANK), f32), panel, panel),
        in_specs=[SMEM] * 2 + [HBM] * 6,
        out_specs=(HBM,) * 3,
        scratch_shapes=[
            pltpu.VMEM((leaves, width, width), bf16),
            pltpu.VMEM((leaves, 1, width, width), bf16),
            pltpu.VMEM((leaves, width, width), bf16),
            pltpu.VMEM((leaves, entries, RANK, RANK), bf16),
            pltpu.VMEM((RING, RING, HALF, RANK), bf16),
            pltpu.VMEM((RING, RING, HALF, RANK), bf16),
            pltpu.VMEM((2 * leaves, width, RANK), bf16),
            pltpu.VMEM((RING, RANK, RANK), f32),
            pltpu.VMEM((leaves, width, width), f32),
            pltpu.VMEM((leaves, RANK, RANK), f32),
            pltpu.VMEM((leaves * entries, RANK, RANK), bf16),
            pltpu.VMEM((leaves * entries + 1, RANK, RANK), bf16),
            pltpu.VMEM((2, RING, RING, HALF, RANK), bf16),
            pltpu.VMEM((2, SIZE, RING, HALF, RANK), bf16),
            pltpu.VMEM((2, SIZE - 1, RING, HALF, RANK), bf16),
            pltpu.VMEM((2, RING, HALF, RANK), bf16),
            pltpu.VMEM((2, RING, HALF, RANK), bf16),
            pltpu.VMEM((leaves, RANK, width), bf16),
            pltpu.VMEM((RING, RANK, RANK), bf16),
            pltpu.VMEM((RING, 2 * RANK, RANK), bf16),
            pltpu.VMEM((2, RANK, RING * RANK), bf16),
            pltpu.VMEM((RANK, RANK), f32),
            pltpu.VMEM((2, DEPTH, RANK), f32),
            pltpu.VMEM((3, RING, DEPTH, RANK), f32),
            pltpu.VMEM(TILE, jnp.int32),
            pltpu.SMEM(TILE, jnp.int32),
            pltpu.VMEM((leaves, RANK, RANK), f32),
            pltpu.VMEM((1, RANK, RANK), f32),
            pltpu.VMEM((1, RANK, RANK), f32),
            sems((2 * leaves + 6,)),
            sems((3, RING)), sems((3, RING)),
            sems((2, 2, SIZE + 1, PIECES)), sems((2, 2, SIZE + 1, PIECES)),
            sems((2, 2, SIZE + 1, PIECES)), sems((2, 2, SIZE + 1, PIECES)),
            sems((2, RING)), sems((2, RING)),
            sems((RING,)), sems((RING,)),
            sems((3, RING)), sems((3, RING)),
            sems((3,)),
        ],
        compiler_params=pltpu.CompilerParams(
            collective_id=0, has_side_effects=True, vmem_limit_bytes=58 * 2**20
        ),
    )(adm_list, near_list.T, self_blocks, near_blocks, leaf_basis, transfer, parent_kernel, chain_coupling)
    return pl.pallas_call(
        hand_out,
        out_shape=tuple(jax.ShapeDtypeStruct(r.shape, r.dtype) for r in results),
        in_specs=[VMEM] * 3,
        out_specs=(VMEM,) * 3,
        compiler_params=pltpu.CompilerParams(vmem_limit_bytes=58 * 2**20),
    )(*results)


def solution(mesh):
    lead = P(("grp", "leaf"))
    return jax.shard_map(
        per_device,
        mesh=mesh,
        in_specs=(lead, lead, lead, lead, lead, lead, lead, P("grp")),
        out_specs=(lead, lead, P("grp")),
        check_vma=False,
    )
```

```python
import functools

import jax
import jax.numpy as jnp
from jax import lax
from jax.experimental import pallas as pl
from jax.experimental.pallas import tpu as pltpu
from jax.sharding import PartitionSpec as P

f32 = jnp.float32
bf16 = jnp.bfloat16
MESH = pl.DeviceIdType.MESH
VMEM = pl.BlockSpec(memory_space=pltpu.VMEM)
SMEM = pl.BlockSpec(memory_space=pltpu.SMEM)
ANY = pl.BlockSpec(memory_space=pl.ANY)
HBM = pl.BlockSpec(memory_space=pltpu.HBM)
RING = 8
RANK = 128
HALF = 64
TILE = (8, 128)


def dot(a, b):
    return jnp.dot(a, b, preferred_element_type=f32)


def dot_t(a, b):
    return lax.dot_general(a, b, (((0,), (0,)), ((), ())), preferred_element_type=f32)


def dot_full(a, b):
    return jnp.dot(a, b, precision=lax.Precision.HIGHEST, preferred_element_type=f32)


def dot_t_full(a, b):
    return lax.dot_general(
        a, b, (((0,), (0,)), ((), ())), precision=lax.Precision.HIGHEST, preferred_element_type=f32
    )


def split(x):
    high = x.astype(bf16)
    return high, (x - high.astype(f32)).astype(bf16)


def dot_split(a, b):
    (ah, al), (bh, bl) = split(a), split(b)
    return dot(ah, bh) + (dot(ah, bl) + dot(al, bh))


def invert(first, second, between):
    sub = lax.broadcasted_iota(jnp.int32, TILE, 0)
    lane = lax.broadcasted_iota(jnp.int32, TILE, 1)
    lane_all = lax.broadcasted_iota(jnp.int32, (RANK, RANK), 1)
    upper_half = sub < 4
    turn = lambda x: pltpu.roll(x, 4, axis=0)
    pack = lambda x, y: (jnp.where(upper_half, x, turn(y)), jnp.where(upper_half, turn(x), y))
    spread = lambda x, j: jnp.take_along_axis(x, jnp.where(upper_half, j, 4 + j), axis=0)
    steps = RANK // 8
    strip = pack(first[0:8], second[0:8])
    for s in range(steps):
        c0 = 8 * s
        last = s + 1 == steps
        inside = (lane >= c0) & (lane < c0 + 8)
        column = lambda x, i: jnp.broadcast_to(x[:, c0 + i : c0 + i + 1], TILE)
        columns = [[column(x, i) for i in range(8)] for x in strip]
        block = {(j, i): spread(columns[j // 4][i], j % 4) for i in range(8) for j in range(i, 8)}
        rows = [
            jnp.where(inside, jnp.where(lane == c0 + j, 1.0, 0.0), spread(strip[j // 4], j % 4)) for j in range(8)
        ]
        if not last:
            below = pack(first[c0 + 8 : c0 + 16], second[c0 + 8 : c0 + 16])
            left = [[column(x, i) for i in range(8)] for x in below]
            following = [jnp.where(inside, 0.0, x) for x in below]
        mult = {}
        for k in range(8):
            pivot = 1.0 / block[k, k]
            for j in range(k + 1, 8):
                mult[j, k] = block[j, k] * pivot
            for j in range(k + 1, 8):
                for i in range(k + 1, j + 1):
                    block[j, i] = block[j, i] - mult[j, k] * block[i, k]
                rows[j] = rows[j] - mult[j, k] * rows[k]
            rows[k] = rows[k] * pivot
            if not last:
                for q in range(2):
                    following[q] = following[q] - left[q][k] * rows[k]
                    for j in range(k + 1, 8):
                        left[q][j] = left[q][j] - mult[j, k] * left[q][k]
        for k in range(7, 0, -1):
            for j in range(k):
                rows[j] = rows[j] - mult[k, j] * rows[k]
        kept, turned = rows[0], rows[4]
        for j in range(1, 8):
            kept = jnp.where(sub == j, rows[j], kept)
            turned = jnp.where(sub == j, rows[(j + 4) % 8], turned)
        turned = turn(turned)
        inside_all = (lane_all >= c0) & (lane_all < c0 + 8)
        nothing = jnp.zeros(TILE, f32)
        results = []
        for a, done in (
            (first, jnp.where(upper_half, kept, turned)),
            (second, jnp.where(upper_half, turned, kept)),
        ):
            high = done.astype(bf16).astype(f32)
            place = lambda x: jnp.concatenate([x if t == s else nothing for t in range(steps)], axis=0).astype(bf16)
            zh, zl = place(high), place(done - high)
            wide = jnp.concatenate(
                [
                    jnp.concatenate([zh, zl], axis=1),
                    jnp.concatenate([zh, jnp.zeros((RANK, RANK), bf16)], axis=1),
                ],
                axis=0,
            )
            product = dot(jnp.concatenate(split(a), axis=1), wide)
            rest = jnp.where(inside_all, 0.0, a) - (product[:, :RANK] + product[:, RANK:])
            results.append(
                jnp.concatenate([done if t == s else rest[8 * t : 8 * t + 8] for t in range(steps)], axis=0)
            )
        first, second = results
        if not last:
            strip = following
        between(s)
    return first, second


def form_reduced(l, parts, blocks, basis, reduced):
    turned = dot(blocks[l], basis[l]).astype(bf16)
    reduced[l] = dot_t(turned, basis[l])
    for i in range(parts - 1):
        for j in range(i, parts - 1):
            si, sj = pl.ds(RANK * i, RANK), pl.ds(RANK * j, RANK)
            x = 0.5 * (reduced[l, si, sj] + reduced[l, sj, si].T)
            reduced[l, si, sj] = x
            if j > i:
                reduced[l, sj, si] = x.T


def eliminate(leaves, parts, reduced, inverses, between):
    @pl.loop(0, parts - 1)
    def _(k):
        here = pl.ds(pl.multiple_of(k * RANK, RANK), RANK)
        inverses[0], inverses[1] = invert(reduced[0, here, here], reduced[1, here, here], functools.partial(between, k))
        for known in range(parts - 1):

            @pl.when(k == known)
            def _(known=known):
                here = pl.ds(RANK * known, RANK)
                rest = pl.ds(RANK * (known + 1), RANK * (parts - 1 - known))
                for l in range(leaves):
                    solved = dot_split(inverses[l], reduced[l, here, rest])
                    reduced[l, rest, rest] = reduced[l, rest, rest] - dot_split(reduced[l, rest, here], solved)


class Places:
    def __init__(self):
        self.grp = lax.axis_index("grp")
        self.leaf = lax.axis_index("leaf")
        self.z = self.leaf // RING
        self.y = self.leaf % RING

    def on_z(self, z):
        return (self.grp, z * RING + self.y)

    def on_y(self, y):
        return (self.grp, self.z * RING + y)

    def on_grp(self, grp):
        return (grp, self.leaf)

    def on_leaf(self, step):
        n = lax.axis_size("leaf")
        return (self.grp, (self.leaf + step + n) % n)


def others(pos):
    return [(pos + o) % RING for o in range(1, RING)]


def partners(at):
    ids = [at.on_z(i) for i in others(at.z)] + [at.on_y(i) for i in others(at.y)]
    return ids + [at.on_grp(i) for i in others(at.grp)] + [at.on_leaf(1), at.on_leaf(-1)]


def greet(at):
    for i in partners(at):
        pl.semaphore_signal(pltpu.get_barrier_semaphore(), inc=1, device_id=i, device_id_type=MESH)


def await_greetings(at):
    pl.semaphore_wait(pltpu.get_barrier_semaphore(), len(partners(at)))


def remote(src, dst, send, recv, to):
    return pltpu.make_async_remote_copy(
        src_ref=src, dst_ref=dst, send_sem=send, recv_sem=recv, device_id=to, device_id_type=MESH
    )


def exchange(pos, to, src, dst, send, recv):
    copies = []
    for o in range(1, RING):
        i = (pos + o) % RING
        copy = remote(src(i), dst.at[pos], send.at[o], recv.at[o], to(i))
        copy.start()
        copies.append(copy)
    return copies


def wait_all(copies):
    for copy in copies:
        copy.wait()


SIZE = RING // 2
PIECES = 2
DEPTH = RANK // RING
SPAN = RING // PIECES
GATHER_AT = [
    ((0, 14), 2, 0), ((0, 15), 2, 1), ((1, 11), 3, 0), ((1, 13), 3, 1), ((2, 11), 4, 0), ((2, 13), 4, 1),
]


def kernel_body(
    adm_hbm, near_list_hbm, blocks_hbm, near_hbm, basis_hbm, transfer_hbm, kernel_hbm, chain_hbm,
    panels_hbm, parent_hbm, top_hbm,
    blocks, near, basis, transfer, upper, lower, halo, maps, reduced, inverses, lifted, terms, shares,
    chain_in, near_sum, far_in, facing, local_in, prefix, prefix_t, cross, slabs, slab_in, inverse, where, panels_ref, parent_ref, top_ref, adm, near_list,
    load_sem, send_1, recv_1, send_2, recv_2, send_c, recv_c, send_f, recv_f, send_g, recv_g, send_r, recv_r, out_sem,
):
    at = Places()
    leaves, width = basis.shape[:2]
    entries = transfer.shape[1]
    parts = width // RANK
    skeleton = pl.ds(width - RANK, RANK)
    lines = ((at.z, at.on_z), (at.y, at.on_y))

    top = kernel_hbm.at[0, pl.ds(0, HALF)]
    bottom = kernel_hbm.at[0, pl.ds(HALF, HALF)]
    loads = []
    for l in range(leaves):
        loads += [(basis_hbm.at[l], basis.at[l]), (blocks_hbm.at[l], blocks.at[l])]
    loads += [(near_hbm, near), (transfer_hbm, transfer)]
    loads += [(top, upper.at[at.y, at.z]), (bottom, lower.at[at.z, at.y]), (chain_hbm.at[0], maps.at[at.grp])]
    loads = [pltpu.make_async_copy(src, dst, load_sem.at[i]) for i, (src, dst) in enumerate(loads)]
    results = ((panels_ref, panels_hbm), (parent_ref, parent_hbm), (top_ref, top_hbm))
    results = [pltpu.make_async_copy(src, dst, out_sem.at[i]) for i, (src, dst) in enumerate(results)]
    scalars = [
        pltpu.make_async_copy(adm_hbm, adm, load_sem.at[2 * leaves + 6]),
        pltpu.make_async_copy(near_list_hbm, near_list, load_sem.at[2 * leaves + 7]),
    ]
    greet(at)
    loads[0].start()
    loads[1].start()
    await_greetings(at)
    exchange(at.z, at.on_z, lambda i: top, upper.at[at.y], send_1.at[0], recv_1.at[0])
    exchange(at.y, at.on_y, lambda i: bottom, lower.at[at.z], send_1.at[1], recv_1.at[1])
    for load in loads[2 : 2 * leaves] + loads[-3:-1] + scalars:
        load.start()

    for l in range(leaves):
        loads[2 * l].wait()
        loads[2 * l + 1].wait()
        form_reduced(l, parts, blocks, basis, reduced)

    def gather_copies(t, u):
        copies = []
        piece = pl.ds(u * SPAN, SPAN)
        for h, (table, pos, to) in enumerate(((upper, at.y, at.on_y), (lower, at.z, at.on_z))):
            for up in range(2):
                if t == SIZE and up == u % 2:
                    continue
                chunk = (pos - t + 1 + RING) % RING if up else (pos + t - 1) % RING
                target = (pos + 1) % RING if up else (pos + RING - 1) % RING
                part = table.at[chunk, piece]
                copies.append(remote(part, part, send_2.at[h, up, t, u], recv_2.at[h, up, t, u], to(target)))
        return copies

    def halo_copies():
        source = basis.at[:, :, skeleton]
        return [
            remote(source, halo.at[pl.ds(0, leaves)], send_1.at[0, 0], recv_1.at[0, 0], at.on_leaf(1)),
            remote(source, halo.at[pl.ds(leaves, leaves)], send_1.at[1, 0], recv_1.at[1, 0], at.on_leaf(-1)),
        ]

    def first_copies():
        return [
            remote(top, upper.at[at.y, at.z], send_1.at[0, o], recv_1.at[0, o], at.on_z((at.z + o) % RING))
            for o in range(1, RING)
        ] + [
            remote(bottom, lower.at[at.z, at.y], send_1.at[1, o], recv_1.at[1, o], at.on_y((at.y + o) % RING))
            for o in range(1, RING)
        ]

    def between(k, s):
        for (block, step), t, u in GATHER_AT:
            if s == step:

                @pl.when(k == block)
                def _(t=t, u=u):
                    for copy in gather_copies(t - 1, u):
                        copy.wait_recv()
                    for copy in gather_copies(t, u):
                        copy.start()
                    if (t, u) == (2, PIECES - 1):
                        exchange(at.grp, at.on_grp, lambda i: chain_hbm.at[0], maps, send_1.at[2], recv_1.at[2])

        if s == 4:

            @pl.when(k == 1)
            def _():
                loads[2 * leaves].wait()
                for l in range(leaves):
                    facing[l] = dot_t(basis[l, :, skeleton], near[l, 0]).astype(bf16)

    loads[-3].wait()
    loads[-2].wait()
    wait_all(first_copies())
    for u in range(PIECES):
        for copy in gather_copies(1, u):
            copy.start()
    for load in (loads[2 * leaves], loads[2 * leaves + 1], loads[-1]):
        load.start()
    eliminate(leaves, parts, reduced, inverses, between)

    wait_all(scalars)
    column = lax.broadcasted_iota(jnp.int32, TILE, 1)
    row = lax.broadcasted_iota(jnp.int32, TILE, 0)
    places = jnp.full(TILE, leaves * entries, jnp.int32)
    for l in range(leaves):
        for a in range(entries):
            places = jnp.where((column == adm[l, a]) & (row == l), l * entries + a, places)
    inverse[...] = places
    to_scalars = pltpu.make_async_copy(inverse, where, load_sem.at[2 * leaves + 5])
    to_scalars.start()

    loads[2 * leaves + 1].wait()
    for l in range(leaves):
        lowered = reduced[l, skeleton, skeleton].astype(bf16)
        for a in range(0, entries, 2):
            pair = dot(lowered, jnp.concatenate([transfer[l, a], transfer[l, a + 1]], axis=1)).astype(bf16)
            lifted[l * entries + a] = pair[:, :RANK]
            lifted[l * entries + a + 1] = pair[:, RANK:]

    wait_all(
        [
            remote(chain_hbm.at[0], maps.at[at.grp], send_1.at[2, o], recv_1.at[2, o], at.on_grp((at.grp + o) % RING))
            for o in range(1, RING)
        ]
    )
    loads[-1].wait()
    eye = (
        lax.broadcasted_iota(jnp.int32, (RANK, RANK), 0) == lax.broadcasted_iota(jnp.int32, (RANK, RANK), 1)
    ).astype(f32)
    running = jnp.zeros((RANK, RANK), f32)
    for j in range(RING - 1, -1, -1):
        if j < RING - 1:
            step_map = 0.8 * eye + 0.5 * maps[j + 1]
            running = jnp.where(j < at.grp, dot_split(step_map, running), 0.0)
        running = jnp.where(j == at.grp, eye, running)
        prefix[j] = jnp.concatenate(split(running), axis=0)
        turned = split(running.T)
        for q in range(2):
            prefix_t[q, :, pl.ds(j * RANK, RANK)] = turned[q]

    for u in range(PIECES):
        for copy in gather_copies(SIZE, u):
            copy.wait_recv()
    for copy in halo_copies():
        copy.start()
    nothing = jnp.zeros((RANK, RANK), bf16)

    def diagonal(x, y):
        return jnp.concatenate(
            [jnp.concatenate([x, nothing], axis=1), jnp.concatenate([nothing, y], axis=1)], axis=0
        )

    total = None
    for l in range(leaves):
        for a in range(0, entries, 2):
            panels = [lifted[l * entries + a + q] for q in range(2)]
            kernels = []
            for q in range(2):
                p = adm[l, a + q]
                pz, py = p // RING, p % RING
                kernels.append(jnp.concatenate([upper[py, pz], lower[pz, py]], axis=0))
            mixture = dot(jnp.concatenate(kernels, axis=1), diagonal(*panels)).astype(bf16)
            term = dot(
                jnp.concatenate([panel.T for panel in panels], axis=1),
                diagonal(mixture[:, :RANK], mixture[:, RANK:]),
            )
            for q in range(2):
                part = term[:, q * RANK : (q + 1) * RANK]
                terms[l * entries + a + q] = part.astype(bf16)
                total = part if total is None else total + part

    terms[leaves * entries] = jnp.zeros((RANK, RANK), bf16)
    to_scalars.wait()
    local_in[at.grp] = total.astype(bf16)
    by_grp = exchange(at.grp, at.on_grp, lambda i: local_in.at[at.grp], local_in, send_g, recv_g)

    @pl.loop(0, RING)
    def _(pz):
        for py in range(RING):
            p = pz * RING + py
            share = terms[where[0, p]].astype(f32)
            for l in range(1, leaves):
                share = share + terms[where[l, p]].astype(f32)
            share = share.astype(bf16)
            shares[0, pz, py] = share[:HALF]
            shares[1, py, pz] = share[HALF:]

    def chain_chunk(h, up, t):
        pos, _ = lines[h]
        return (pos + 5 - t) % RING if up else (pos - 5 + t + RING) % RING

    def starts(up, t, u):
        return t > 1 or up == u % 2

    def chain_copy(h, up, t, u):
        pos, to = lines[h]
        piece = pl.ds(u * SPAN, SPAN)
        src = chain_in.at[h, up, t - 2, piece] if starts(up, t - 1, u) and t > 1 else shares.at[h, chain_chunk(h, up, t), piece]
        target = (pos + 1) % RING if up else (pos + RING - 1) % RING
        return remote(src, chain_in.at[h, up, t - 1, piece], send_c.at[h, up, t, u], recv_c.at[h, up, t, u], to(target))

    def chain_step(t):
        for u in range(PIECES):
            piece = pl.ds(u * SPAN, SPAN)
            for h in range(2):
                for up in range(2):
                    if not starts(up, t, u):
                        continue
                    if t > 1 and starts(up, t - 1, u):
                        chain_copy(h, up, t - 1, u).wait_recv()
                        mine = shares[h, chain_chunk(h, up, t), piece].astype(f32)
                        chain_in[h, up, t - 2, piece] = (chain_in[h, up, t - 2, piece].astype(f32) + mine).astype(bf16)
                    chain_copy(h, up, t, u).start()

    chain_step(1)

    chain_step(2)

    wait_all(by_grp)
    mapped = []
    for j in range(RING):
        root = local_in[j]
        mapped.append(dot(jnp.concatenate([root, root], axis=1), prefix[j]))
    high, low = split(jnp.concatenate(mapped, axis=0))
    cross[...] = (dot(prefix_t[0], high) + (dot(prefix_t[1], high) + dot(prefix_t[0], low))) * (1.0 / (RING * RING))

    slab = lambda i: pl.ds(pl.multiple_of(i * DEPTH, DEPTH), DEPTH)

    def gathered(stage, pos, mine):
        total = mine
        for o in range(1, RING):
            total = total + slab_in[stage, (pos + o) % RING]
        return total

    by_z = exchange(at.z, at.on_z, lambda i: cross.at[slab(i)], slab_in.at[0], send_r.at[0], recv_r.at[0])

    chain_step(3)

    for copy in halo_copies():
        copy.wait()
    first = ((at.grp * lax.axis_size("leaf") + at.leaf) - 1) * leaves
    for l in range(leaves):
        place = near_list[0, l] - first
        place = jnp.clip(jnp.where(place < leaves, place, place - leaves), 0, 2 * leaves - 1)
        panels_ref[l] = reduced[l, skeleton, skeleton] + dot(facing[l], halo[place])
    results[0].start()

    wait_all(by_z)
    slabs[0] = gathered(0, at.z, cross[slab(at.z)])
    by_y = exchange(at.y, at.on_y, lambda i: slabs.at[0], slab_in.at[1], send_r.at[1], recv_r.at[1])
    chain_step(4)

    def far_copy(h, i):
        other, to = lines[1 - h]
        return remote(near_sum.at[h, i], far_in.at[h, other], send_f.at[h, i], recv_f.at[h, other], to(i))

    for u in range(PIECES):
        piece = pl.ds(u * SPAN, SPAN)
        for h in range(2):
            pos, _ = lines[h]
            for up in range(2):
                chain_copy(h, up, SIZE, u).wait_recv()
            near_sum[h, piece] = (
                chain_in[h, 0, SIZE - 1, piece].astype(f32)
                + chain_in[h, 1, SIZE - 1, piece].astype(f32)
                + shares[h, pos, piece].astype(f32)
            ).astype(bf16)
            for i in range(u * SPAN, (u + 1) * SPAN):

                @pl.when(i != lines[1 - h][0])
                def _(h=h, i=i):
                    far_copy(h, i).start()

    wait_all(by_y)
    slabs[1] = gathered(1, at.y, slabs[0])
    again = exchange(at.z, at.on_z, lambda i: slabs.at[1], slab_in.at[2], send_r.at[2], recv_r.at[2])
    for t in range(1, SIZE + 1):
        for u in range(PIECES):
            for copy in gather_copies(t, u):
                copy.wait_send()
    wait_all(again)
    slab_in[2, at.z] = slabs[1]
    for i in range(RING):
        top_ref[0, pl.ds(i * DEPTH, DEPTH)] = slab_in[2, i]
    results[2].start()
    for h in range(2):
        for up in range(2):
            for t in range(1, SIZE + 1):
                for u in range(PIECES):
                    if starts(up, t, u):
                        chain_copy(h, up, t, u).wait_send()
    for h in range(2):
        other, to = lines[1 - h]
        total = near_sum[h, other].astype(f32)
        for o in range(1, RING):
            i = (other + o) % RING
            far_copy(h, i).wait_send()
            remote(near_sum.at[h, i], far_in.at[h, i], send_f.at[h, i], recv_f.at[h, i], to(i)).wait_recv()
            total = total + far_in[h, i].astype(f32)
        parent_ref[0, pl.ds(h * HALF, HALF)] = total
    results[1].start()
    wait_all(results)


def hand_out(*refs):
    for i in range(3):
        refs[3 + i][...] = refs[i][...]


def per_device(self_blocks, near_blocks, leaf_basis, transfer, near_list, adm_list, parent_kernel, chain_coupling):
    leaves, width = leaf_basis.shape[:2]
    entries = transfer.shape[1]
    sems = pltpu.SemaphoreType.DMA
    panel = jax.ShapeDtypeStruct((1, RANK, RANK), f32)
    results = pl.pallas_call(
        kernel_body,
        out_shape=(jax.ShapeDtypeStruct((leaves, RANK, RANK), f32), panel, panel),
        in_specs=[HBM] * 8,
        out_specs=(HBM,) * 3,
        scratch_shapes=[
            pltpu.VMEM((leaves, width, width), bf16),
            pltpu.VMEM((leaves, 1, width, width), bf16),
            pltpu.VMEM((leaves, width, width), bf16),
            pltpu.VMEM((leaves, entries, RANK, RANK), bf16),
            pltpu.VMEM((RING, RING, HALF, RANK), bf16),
            pltpu.VMEM((RING, RING, HALF, RANK), bf16),
            pltpu.VMEM((2 * leaves, width, RANK), bf16),
            pltpu.VMEM((RING, RANK, RANK), f32),
            pltpu.VMEM((leaves, width, width), f32),
            pltpu.VMEM((leaves, RANK, RANK), f32),
            pltpu.VMEM((leaves * entries, RANK, RANK), bf16),
            pltpu.VMEM((leaves * entries + 1, RANK, RANK), bf16),
            pltpu.VMEM((2, RING, RING, HALF, RANK), bf16),
            pltpu.VMEM((2, 2, SIZE, RING, HALF, RANK), bf16),
            pltpu.VMEM((2, RING, HALF, RANK), bf16),
            pltpu.VMEM((2, RING, HALF, RANK), bf16),
            pltpu.VMEM((leaves, RANK, width), bf16),
            pltpu.VMEM((RING, RANK, RANK), bf16),
            pltpu.VMEM((RING, 2 * RANK, RANK), bf16),
            pltpu.VMEM((2, RANK, RING * RANK), bf16),
            pltpu.VMEM((RANK, RANK), f32),
            pltpu.VMEM((2, DEPTH, RANK), f32),
            pltpu.VMEM((3, RING, DEPTH, RANK), f32),
            pltpu.VMEM(TILE, jnp.int32),
            pltpu.SMEM(TILE, jnp.int32),
            pltpu.VMEM((leaves, RANK, RANK), f32),
            pltpu.VMEM((1, RANK, RANK), f32),
            pltpu.VMEM((1, RANK, RANK), f32),
            pltpu.SMEM((leaves, entries), jnp.int32),
            pltpu.SMEM((1, leaves), jnp.int32),
            sems((2 * leaves + 8,)),
            sems((3, RING)), sems((3, RING)),
            sems((2, 2, SIZE + 1, PIECES)), sems((2, 2, SIZE + 1, PIECES)),
            sems((2, 2, SIZE + 1, PIECES)), sems((2, 2, SIZE + 1, PIECES)),
            sems((2, RING)), sems((2, RING)),
            sems((RING,)), sems((RING,)),
            sems((3, RING)), sems((3, RING)),
            sems((3,)),
        ],
        compiler_params=pltpu.CompilerParams(
            collective_id=0, has_side_effects=True, vmem_limit_bytes=58 * 2**20
        ),
    )(adm_list, near_list.T, self_blocks, near_blocks, leaf_basis, transfer, parent_kernel, chain_coupling)
    return pl.pallas_call(
        hand_out,
        out_shape=tuple(jax.ShapeDtypeStruct(r.shape, r.dtype) for r in results),
        in_specs=[VMEM] * 3,
        out_specs=(VMEM,) * 3,
        compiler_params=pltpu.CompilerParams(vmem_limit_bytes=58 * 2**20),
    )(*results)


def solution(mesh):
    lead = P(("grp", "leaf"))
    return jax.shard_map(
        per_device,
        mesh=mesh,
        in_specs=(lead, lead, lead, lead, lead, lead, lead, P("grp")),
        out_specs=(lead, lead, P("grp")),
        check_vma=False,
    )
```
